128 devices in a mesh: line: 8 (over y, core), track: 16 (over x, z).
Axes of the slice: x: 4, y: 4, z: 4, core: 2. Of those that a mesh axis runs over, the one named last changes fastest.
Arguments:
- radiance: bfloat16 [8, 425, 256, 384], P('line', None, 'track')
- counts: int32 [8, 16], P('line', 'track'), may hold values from 4 to 16, as said below
- start: float32 [425, 64], replicated, may hold values from -0.3125 to 0.3125
Outputs:
- projector: float32 [425, 425], replicated
- scores: float32 [8, 64, 256, 384], P('line', None, 'track')
The draws below stay inside these ranges and needn't reach their ends.
Inputs may be any that keep to these rules, and one draw needn't show every extreme that they name: `counts`: every tile has at least 4 valid rows, and at least one tile is wholly valid.
All inputs are finite; a program needn't handle non-finite values.
Results may differ from the reference program's by a relative error of at most 0.0024.
The reference program's roundings to bfloat16 on the way (of `features`) count: a program that leaves them out, or rounds other values in their place, can miss the bound.
Values may be sent and summed in bfloat16 or wider, within the bound.
A program may use at most 128 MiB of HBM per device.

```python
import math
import jax
import jax.numpy as jnp
from jax import lax

BANDS = 425
RANK = 64
ITERS = 6
ROWS_DEV = 16
COLS = 384
LINES = 8
TILES = 16
ROWS = 256


def draw_radiance(key, part):
    keys = jax.random.split(key, 3)
    shape = (LINES, BANDS, ROWS, COLS)
    band_scale = jnp.exp(jax.random.uniform(keys[0], (1, BANDS, 1, 1), jnp.float32, math.log(0.1), 0.0))
    pixel_scale = jnp.exp(jax.random.uniform(keys[1], (LINES, 1, ROWS, COLS), jnp.float32, math.log(0.5), math.log(2.0)))
    values = band_scale * pixel_scale * jax.random.normal(keys[2], shape, jnp.float32)
    return values.astype(jnp.bfloat16)


def draw_counts(key, part):
    keys = jax.random.split(key, 3)
    raw = jax.random.randint(keys[0], (LINES, TILES), ROWS_DEV // 4, ROWS_DEV * 3 // 2 + 1)
    capped = jnp.minimum(raw, ROWS_DEV)
    line_pick = jax.random.randint(keys[1], (), 0, LINES)
    tile_pick = jax.random.randint(keys[2], (), 0, TILES)
    return capped.at[line_pick, tile_pick].set(ROWS_DEV).astype(jnp.int32)


def gaussian(own_key, extent, scale, most, kind=jnp.bfloat16):
    values = jax.random.normal(own_key, extent, jnp.float32) * scale
    return jnp.minimum(jnp.maximum(values, -most), most).astype(kind)


def setup_inputs(seed: int = 0) -> dict:
    key_of = jax.random.split(jax.random.key(seed), 4)
    radiance = draw_radiance(jax.random.fold_in(key_of[3], 71), 0)
    counts = draw_counts(jax.random.fold_in(key_of[3], 71), 0)
    start = gaussian(key_of[2], (BANDS, RANK), BANDS ** -0.5, 0.3125, jnp.float32)
    return dict(radiance=radiance, counts=counts, start=start)


def make_features(padded, valid):
    rows_out = padded.shape[1] - 4
    smooth = (padded[:, 0:rows_out] + 4.0 * padded[:, 1:rows_out + 1] + 6.0 * padded[:, 2:rows_out + 2] + 4.0 * padded[:, 3:rows_out + 3] + padded[:, 4:rows_out + 4]) / 16.0
    cols_out = smooth.shape[2]
    wide = jnp.pad(smooth, ((0, 0), (0, 0), (2, 2)))
    smooth = (wide[:, :, 0:cols_out] + 4.0 * wide[:, :, 1:cols_out + 1] + 6.0 * wide[:, :, 2:cols_out + 2] + 4.0 * wide[:, :, 3:cols_out + 3] + wide[:, :, 4:cols_out + 4]) / 16.0
    banded = jnp.pad(smooth, ((1, 1), (0, 0), (0, 0)))
    derived = 0.5 * (banded[2:] - banded[:-2]) * valid[None, :, None]
    return derived.astype(jnp.bfloat16).reshape(derived.shape[0], -1)

def orthonormal(block):
    inner = jnp.dot(block.T, block, precision=lax.Precision.HIGHEST)
    factor = jnp.linalg.cholesky(inner)
    return lax.linalg.triangular_solve(factor, block, left_side=False, lower=True, transpose_a=True)

def line_features(cube, line_counts):
    limits = jnp.repeat(line_counts, ROWS_DEV)
    local_rows = jnp.arange(ROWS, dtype=jnp.int32) % ROWS_DEV
    valid = (local_rows < limits).astype(jnp.float32)
    masked = cube.astype(jnp.float32) * valid[None, :, None]
    padded = jnp.pad(masked, ((0, 0), (2, 2), (0, 0)))
    return make_features(padded, valid)

def reference(radiance, counts, start):

    def accumulate(total, pair):
        features = line_features(pair[0], pair[1])
        return (total + jnp.dot(features.astype(jnp.float32), features.T.astype(jnp.float32), preferred_element_type=jnp.float32), None)
    gram, unused = lax.scan(accumulate, jnp.zeros((BANDS, BANDS), jnp.float32), (radiance, counts))
    basis = orthonormal(start)
    for iteration in range(ITERS):
        basis = orthonormal(jnp.dot(gram, basis, precision=lax.Precision.HIGHEST))
    projector = jnp.dot(basis, basis.T, precision=lax.Precision.HIGHEST)
    narrow = basis.astype(jnp.bfloat16)

    def project(pair):
        features = line_features(pair[0], pair[1])
        return jnp.dot(narrow.T.astype(jnp.float32), features.astype(jnp.float32), preferred_element_type=jnp.float32).reshape(RANK, ROWS, COLS)
    scores = lax.map(project, (radiance, counts))
    return (projector, scores)
```

```python
import functools

import jax
import jax.numpy as jnp
from jax import lax
from jax.experimental import pallas as pl
from jax.experimental.pallas import tpu as pltpu
from jax.sharding import PartitionSpec as P

MESH = pl.DeviceIdType.MESH
F32 = jnp.float32
BF16 = jnp.bfloat16

BANDS = 425
BP = 432
GROUPS = BP // 16
RANK = 64
ITERS = 6
ROWS = 16
COLS = 384
TILES = 16
CHUNK = 3
CHUNKS = GROUPS // CHUNK
HR = 16 + 2 * BP + 16
EDGE = (0, 1, 14, 15)
BIN = lambda dist: jnp.where(dist == 0, 6.0, jnp.where(dist == 1, 4.0, jnp.where(dist == 2, 1.0, 0.0)))
NT = (((1,), (1,)), ((), ()))
LOWER = [(rt, ct) for ct in range(4) for rt in range(16 * ct, BP // 8)]


def iotas(shape):
    return lax.broadcasted_iota(jnp.int32, shape, 0), lax.broadcasted_iota(jnp.int32, shape, 1)


def smooth_cols(t):
    rows = t.shape[0]
    lane = lax.broadcasted_iota(jnp.int32, (rows, 128), 1)
    first, last = lane == 0, lane == 127
    x = [t[:, 128 * i : 128 * i + 128] for i in range(3)]

    def right(v, edge):
        r = [pltpu.roll(a, 1, 1) for a in v]
        return [jnp.where(first, p, a) for p, a in zip([edge] + r[:2], r)]

    def left(v, edge):
        r = [pltpu.roll(a, 127, 1) for a in v]
        return [jnp.where(last, n, a) for n, a in zip(r[1:] + [edge], r)]

    zero = jnp.zeros((rows, 128), F32)
    v = [a + b for a, b in zip(x, right(x, zero))]
    y = [a + b for a, b in zip(v, left(v, x[2]))]
    w = [a + b for a, b in zip(y, right(y, x[0]))]
    return [a + b for a, b in zip(w, left(w, x[2] + y[2]))]


def features_kernel(
    counts_ref, x_hbm, f_hbm, g_ref,
    xs, su, sd, hu, hd, fs, tb, gs, pk, r1, r2, ag,
    x_sem, f_sem, su_sem, sd_sem, hu_sem, hd_sem, ex_send, ex_recv,
):
    line, track = lax.axis_index("line"), lax.axis_index("track")
    y, core = line // 2, line % 2
    xx, z = track // 4, track % 4
    chip = 16 * xx + 4 * y + z
    sibling = (2 * y + 1 - core, track)

    def peer(d):
        px, py, pz = (xx + d // 16) % 4, (y + (d // 4) % 4) % 4, (z + d % 4) % 4
        return 16 * px + 4 * py + pz, (2 * py + core, 4 * px + pz)

    crow = 256 * CHUNK

    def load(j):
        n = crow if j < CHUNKS - 1 else ROWS * BANDS - crow * (CHUNKS - 1)
        return pltpu.make_async_copy(
            x_hbm.at[pl.ds(crow * j, n)], xs.at[pl.ds(16 + crow * j, n)], x_sem.at[j]
        )

    for j in range(CHUNKS):
        load(j).start()

    barrier = pltpu.get_barrier_semaphore()
    pl.semaphore_signal(barrier, inc=1, device_id=sibling, device_id_type=MESH)

    def greet(d, carry):
        pl.semaphore_signal(barrier, inc=1, device_id=peer(d)[1], device_id_type=MESH)
        return carry

    lax.fori_loop(1, 64, greet, 0)

    xs[0:16, :] = jnp.zeros((16, COLS), BF16)
    tail = ROWS * (BANDS + 1)
    xs[tail : ROWS * (BP + 2), :] = jnp.zeros((ROWS * (BP + 2) - tail, COLS), BF16)
    for h in (hu, hd):
        h[0:16, :] = jnp.zeros((16, COLS), BF16)
        h[HR - 16 : HR, :] = jnp.zeros((16, COLS), BF16)
    gs[:, 384:512] = jnp.zeros((BP, 128), F32)

    cnt = counts_ref[0, 0]
    ri, ci = iotas((64, 256))
    want = jnp.where(ri < 32, ri & 1, 14 + (ri & 1))
    sel = ((((ri & 31) >> 1) == (ci >> 4)) & (want == (ci & 15)) & (want < cnt)).astype(F32).astype(BF16)

    ri, ci = iotas((128, 160))
    r, b, bi, rr = ri >> 3, ri & 7, ci >> 4, ci & 15
    sign = (bi == b + 2).astype(F32) - (bi == b).astype(F32)
    wt = jnp.where((r < cnt) & (rr < cnt), BIN(jnp.abs(rr - r)), 0.0)
    body = (sign * wt * (1.0 / 512.0)).astype(BF16)

    ri, ci = iotas((64, 128))
    q, b = ri >> 4, ri & 15
    r = jnp.where(q < 2, q, q + 12)
    up = ci < 64
    cj = ci & 63
    bi, rr = cj >> 1, jnp.where(up, (cj & 1) - 2, (cj & 1) + 16)
    sign = (bi == b + 9).astype(F32) - (bi == b + 7).astype(F32)
    have = jnp.where(up, track, TILES - 1 - track) > 0
    wt = jnp.where((r < cnt) & have, BIN(jnp.abs(rr - r)), 0.0)
    rim = (sign * wt * (1.0 / 512.0)).astype(BF16)

    def halo(j):
        rows = pl.ds(pl.multiple_of(16 + 32 * CHUNK * j, 32 * CHUNK // 6), 32 * CHUNK)
        first = pltpu.make_async_remote_copy(
            src_ref=su.at[rows], dst_ref=hd.at[rows], send_sem=su_sem.at[j], recv_sem=hd_sem.at[j],
            device_id=(line, (track + TILES - 1) % TILES), device_id_type=MESH,
        )
        last = pltpu.make_async_remote_copy(
            src_ref=sd.at[rows], dst_ref=hu.at[rows], send_sem=sd_sem.at[j], recv_sem=hu_sem.at[j],
            device_id=(line, (track + 1) % TILES), device_id_type=MESH,
        )
        return first, last

    for j in range(CHUNKS):
        load(j).wait()
        for g in range(CHUNK * j, CHUNK * j + CHUNK):
            picked = jnp.dot(sel, xs[16 + 256 * g : 272 + 256 * g, :], preferred_element_type=F32).astype(BF16)
            su[16 + 32 * g : 48 + 32 * g, :] = picked[0:32]
            sd[16 + 32 * g : 48 + 32 * g, :] = picked[32:64]
        if j == 0:
            pl.semaphore_wait(barrier, 64)
        for copy in halo(j):
            copy.start()

    def interior(g):
        at = pl.multiple_of(16 * g, 16)
        halves = []
        for h in range(2):
            xk = xs[pl.ds(pl.multiple_of(256 * g + 128 * h, 128), 160), :]
            t = jnp.dot(body, xk, preferred_element_type=F32)
            for e, row in enumerate(EDGE):
                tb[e, pl.ds(pl.multiple_of(at + 8 * h, 8), 8), :] = t[8 * row : 8 * row + 8]
            halves.append(smooth_cols(t[16:112]))
        for row in range(2, 14):
            k = 8 * (row - 2)
            for i in range(3):
                both = jnp.concatenate([halves[0][i][k : k + 8], halves[1][i][k : k + 8]], axis=0)
                col = row * COLS + 128 * i
                fs[pl.ds(at, 16), col : col + 128] = both.astype(BF16)

    def interior_step(s, carry):
        for u in range(3):
            interior(3 * s + u)
        return carry

    lax.fori_loop(0, GROUPS // 3, interior_step, 0)

    def outer(lo, hi):
        a = fs[:, lo:hi]
        left = lax.dot_general(a, a[0:256], NT, preferred_element_type=F32)
        right = lax.dot_general(a[256:BP], a[256:BP], NT, preferred_element_type=F32)
        return left, right

    left, right = outer(2 * COLS, 6 * COLS)
    gs[:, 0:256] = left
    gs[256:BP, 256:BP] = right
    for k in (6, 10):
        left, right = outer(k * COLS, (k + 4) * COLS)
        gs[:, 0:256] += left
        gs[256:BP, 256:BP] += right

    def edge(g):
        at = pl.multiple_of(16 * g, 16)
        src = pl.ds(pl.multiple_of(32 * g, 32), 64)
        halos = jnp.concatenate([hu[src, :], hd[src, :]], axis=0)
        t = jnp.dot(rim, halos, preferred_element_type=F32) + tb[:, pl.ds(at, 16), :].reshape(64, COLS)
        out = smooth_cols(t)
        for e, row in enumerate(EDGE):
            for i in range(3):
                col = row * COLS + 128 * i
                fs[pl.ds(at, 16), col : col + 128] = out[i][16 * e : 16 * e + 16].astype(BF16)

    def edge_step(j, carry):
        for copy in halo(j):
            copy.wait_recv()
        for u in (-1, 0, 1):
            edge(CHUNK * j + u)
        return carry

    for copy in halo(0):
        copy.wait_recv()
    edge(0)
    edge(1)
    lax.fori_loop(1, CHUNKS, edge_step, 0)
    edge(GROUPS - 1)

    f_copy = pltpu.make_async_copy(fs, f_hbm, f_sem)
    f_copy.start()

    for k in (0, 14):
        left, right = outer(k * COLS, (k + 2) * COLS)
        gs[:, 0:256] += left
        gs[256:BP, 256:BP] += right

    for t, (rt, ct) in enumerate(LOWER):
        pk[t] = gs[8 * rt : 8 * rt + 8, 128 * ct : 128 * ct + 128]
    for t in range(len(LOWER), 128):
        pk[t] = jnp.zeros((8, 128), F32)

    mine, other = pl.ds(64 * core, 64), pl.ds(64 * (1 - core), 64)
    pair = pltpu.make_async_remote_copy(
        src_ref=pk.at[other], dst_ref=r1, send_sem=ex_send.at[0], recv_sem=ex_recv.at[0],
        device_id=sibling, device_id_type=MESH,
    )
    pair.start()
    pair.wait_recv()
    pk[mine] += r1[...]

    def scatter(d, carry):
        to, device = peer(d)
        pltpu.make_async_remote_copy(
            src_ref=pk.at[64 * core + to], dst_ref=r2.at[d - 1], send_sem=ex_send.at[1], recv_sem=ex_recv.at[1],
            device_id=device, device_id_type=MESH,
        ).start()
        return carry

    lax.fori_loop(1, 64, scatter, 0)
    pltpu.make_async_copy(r2, r2, ex_recv.at[1]).wait()
    ag[64 * core + chip] = pk[64 * core + chip] + jnp.sum(r2[...], axis=0)

    def gather(d, carry):
        device = peer(d)[1]
        tile = ag.at[64 * core + chip]
        pltpu.make_async_remote_copy(
            src_ref=tile, dst_ref=tile, send_sem=ex_send.at[2], recv_sem=ex_recv.at[2],
            device_id=device, device_id_type=MESH,
        ).start()
        return carry

    lax.fori_loop(1, 64, gather, 0)
    pltpu.make_async_copy(r2, r2, ex_recv.at[2]).wait()
    swap = pltpu.make_async_remote_copy(
        src_ref=ag.at[mine], dst_ref=ag.at[mine], send_sem=ex_send.at[3], recv_sem=ex_recv.at[3],
        device_id=sibling, device_id_type=MESH,
    )
    swap.start()
    swap.wait_recv()
    g_ref[...] = ag[...]

    swap.wait_send()
    pair.wait_send()
    pltpu.make_async_copy(r2, r2, ex_send.at[1]).wait()
    pltpu.make_async_copy(r2, r2, ex_send.at[2]).wait()

    def sent(j, carry):
        for copy in halo(j):
            copy.wait_send()
        return carry

    lax.fori_loop(0, CHUNKS, sent, 0)
    f_copy.wait()


def split3(a):
    hi = a.astype(BF16)
    rest = a - hi.astype(F32)
    mid = rest.astype(BF16)
    low = (rest - mid.astype(F32)).astype(BF16)
    return hi, mid, low


def dot6(a, b, dims):
    n = a.shape[0]
    parts = jnp.concatenate(split3(a), axis=0)
    one = lax.dot_general(parts, b[0], dims, preferred_element_type=F32)
    two = lax.dot_general(parts[: 2 * n], b[1], dims, preferred_element_type=F32)
    three = lax.dot_general(parts[:n], b[2], dims, preferred_element_type=F32)
    return one[:n] + (((one[2 * n :] + two[n:]) + three) + (one[n : 2 * n] + two[:n]))


NN = (((1,), (0,)), ((), ()))


def inverse_factor(s):
    ri, ci = iotas((8, 128))
    blocks = [s[8 * i : 8 * i + 8] + (ci == ri + 64 + 8 * i).astype(F32) for i in range(8)]
    for j in range(RANK):
        pb, pr = divmod(j, 8)
        col = blocks[pb][:, j : j + 1]
        scaled = (blocks[pb] * (1.0 / col))[pr : pr + 1]
        for i in range(pb, 8):
            c = blocks[i][:, j : j + 1]
            if i == pb:
                if pr == 7:
                    continue
                c = jnp.where(ri[:, 0:1] > pr, c, 0.0)
            blocks[i] = blocks[i] - c * scaled
    out = []
    for i in range(8):
        diag = jnp.sum(jnp.where(ci == ri + 8 * i, blocks[i], 0.0), axis=1, keepdims=True)
        out.append(blocks[i] * lax.rsqrt(diag))
    return jnp.concatenate(out, axis=0)


def iterate_kernel(g_ref, start_ref, f_hbm, proj_ref, scores_hbm, gf, gh, gm, gl, tt, fs, sc, f_sem, o_sem):
    f_copy = pltpu.make_async_copy(f_hbm, fs, f_sem)
    f_copy.start()

    gf[BP:512, :] = jnp.zeros((512 - BP, 512), F32)
    for t, (rt, ct) in enumerate(LOWER):
        tile = g_ref[t]
        if rt == 53 or ct == 3:
            ri, ci = iotas((8, 128))
            tile = jnp.where((ri + 8 * rt < BANDS) & (ci + 128 * ct < BANDS), tile, 0.0)
        gf[8 * rt : 8 * rt + 8, 128 * ct : 128 * ct + 128] = tile
    for i in range(4):
        for j in range(i):
            gf[128 * j : 128 * j + 128, 128 * i : 128 * i + 128] = gf[
                128 * i : 128 * i + 128, 128 * j : 128 * j + 128
            ].T
    for ref, part in zip((gh, gm, gl), split3(gf[...])):
        ref[...] = part

    tt[:, 384:512] = jnp.zeros((RANK, 128), F32)
    tt[:, 0:BANDS] = start_ref[...].T

    zeros = jnp.zeros((RANK, 512), BF16)

    def normaliser(t):
        h, m, l = split3(t)
        rhs = tuple(jnp.concatenate([p, zeros], axis=0) for p in (h, m, l))
        return inverse_factor(dot6(t, rhs, NT))

    def apply(w, t):
        rhs = tuple(jnp.concatenate([zeros, p], axis=0) for p in split3(t))
        return dot6(w, rhs, NN)

    def step(i, carry):
        t = tt[...]
        z = dot6(t, (gh[...], gm[...], gl[...]), NN)
        tt[...] = apply(normaliser(t), z)
        return carry

    lax.fori_loop(0, ITERS, step, 0)
    t = tt[...]
    basis = apply(normaliser(t), t)

    h, m, l = split3(basis)
    lhs = jnp.concatenate([h, h, m, m], axis=0).astype(F32).T.astype(BF16)
    rhs = jnp.concatenate([h, m, h, m], axis=0)
    proj = jnp.dot(lhs, rhs, preferred_element_type=F32)
    proj_ref[...] = proj[0:BANDS, 0:BANDS]

    f_copy.wait()
    narrow = h[:, 0:BP]

    def score(r, carry):
        cols = pl.ds(pl.multiple_of(r * COLS, 128), COLS)
        s = jnp.dot(narrow, fs[:, cols], preferred_element_type=F32)
        for i in range(3):
            sc[pl.ds(RANK * ROWS * i + r, RANK, stride=ROWS), :] = s[:, 128 * i : 128 * i + 128]
        return carry

    lax.fori_loop(0, ROWS, score, 0)
    out = [
        pltpu.make_async_copy(
            sc.at[pl.ds(RANK * ROWS * i, RANK * ROWS)], scores_hbm.at[:, pl.ds(128 * i, 128)], o_sem.at[i]
        )
        for i in range(3)
    ]
    for copy in out:
        copy.start()
    for copy in out:
        copy.wait()


def on_device(radiance, counts, start):
    x = radiance.reshape(BANDS * ROWS, COLS)
    vmem = pl.BlockSpec(memory_space=pltpu.VMEM)
    anym = pl.BlockSpec(memory_space=pl.ANY)
    dma = pltpu.SemaphoreType.DMA
    features, tiles = pl.pallas_call(
        features_kernel,
        out_shape=(
            jax.ShapeDtypeStruct((BP, ROWS * COLS), BF16),
            jax.ShapeDtypeStruct((128, 8, 128), F32),
        ),
        in_specs=[pl.BlockSpec(memory_space=pltpu.SMEM), anym],
        out_specs=(anym, vmem),
        scratch_shapes=[
            pltpu.VMEM((ROWS * (BP + 2), COLS), BF16),
            pltpu.VMEM((HR, COLS), BF16),
            pltpu.VMEM((HR, COLS), BF16),
            pltpu.VMEM((HR, COLS), BF16),
            pltpu.VMEM((HR, COLS), BF16),
            pltpu.VMEM((BP, ROWS * COLS), BF16),
            pltpu.VMEM((4, BP, COLS), F32),
            pltpu.VMEM((BP, 512), F32),
            pltpu.VMEM((128, 8, 128), F32),
            pltpu.VMEM((64, 8, 128), F32),
            pltpu.VMEM((63, 8, 128), F32),
            pltpu.VMEM((128, 8, 128), F32),
            dma((CHUNKS,)),
            dma,
            dma((CHUNKS,)),
            dma((CHUNKS,)),
            dma((CHUNKS,)),
            dma((CHUNKS,)),
            dma((4,)),
            dma((4,)),
        ],
        compiler_params=pltpu.CompilerParams(
            collective_id=0, has_side_effects=True, vmem_limit_bytes=48 * 2**20
        ),
    )(counts, x)
    projector, scores = pl.pallas_call(
        iterate_kernel,
        out_shape=(
            jax.ShapeDtypeStruct((BANDS, BANDS), F32),
            jax.ShapeDtypeStruct((RANK * ROWS, COLS), F32),
        ),
        in_specs=[vmem, vmem, anym],
        out_specs=(vmem, anym),
        scratch_shapes=[
            pltpu.VMEM((512, 512), F32),
            pltpu.VMEM((512, 512), BF16),
            pltpu.VMEM((512, 512), BF16),
            pltpu.VMEM((512, 512), BF16),
            pltpu.VMEM((RANK, 512), F32),
            pltpu.VMEM((BP, ROWS * COLS), BF16),
            pltpu.VMEM((3 * RANK * ROWS, 128), F32),
            dma,
            dma((3,)),
        ],
        compiler_params=pltpu.CompilerParams(vmem_limit_bytes=48 * 2**20),
    )(tiles, start, features)
    return projector, scores.reshape(1, RANK, ROWS, COLS)


def solution(mesh):
    return jax.shard_map(
        on_device,
        mesh=mesh,
        in_specs=(P("line", None, "track", None), P("line", "track"), P()),
        out_specs=(P(), P("line", None, "track", None)),
        check_vma=False,
    )
```

```python
import functools

import jax
import jax.numpy as jnp
from jax import lax
from jax.experimental import pallas as pl
from jax.experimental.pallas import tpu as pltpu
from jax.sharding import PartitionSpec as P

MESH = pl.DeviceIdType.MESH
F32 = jnp.float32
BF16 = jnp.bfloat16

BANDS = 425
BP = 432
GROUPS = BP // 16
RANK = 64
ITERS = 6
ROWS = 16
COLS = 384
TILES = 16
CHUNK = 3
CHUNKS = GROUPS // CHUNK
HR = 16 + 2 * BP + 16
EDGE = (0, 1, 14, 15)
BIN = lambda dist: jnp.where(dist == 0, 6.0, jnp.where(dist == 1, 4.0, jnp.where(dist == 2, 1.0, 0.0)))
NT = (((1,), (1,)), ((), ()))
LOWER = [(rt, ct) for ct in range(4) for rt in range(16 * ct, BP // 8)]


def iotas(shape):
    return lax.broadcasted_iota(jnp.int32, shape, 0), lax.broadcasted_iota(jnp.int32, shape, 1)


def smooth_cols(t):
    rows = t.shape[0]
    lane = lax.broadcasted_iota(jnp.int32, (rows, 128), 1)
    first, last = lane == 0, lane == 127
    x = [t[:, 128 * i : 128 * i + 128] for i in range(3)]

    def right(v, edge):
        r = [pltpu.roll(a, 1, 1) for a in v]
        return [jnp.where(first, p, a) for p, a in zip([edge] + r[:2], r)]

    def left(v, edge):
        r = [pltpu.roll(a, 127, 1) for a in v]
        return [jnp.where(last, n, a) for n, a in zip(r[1:] + [edge], r)]

    zero = jnp.zeros((rows, 128), F32)
    v = [a + b for a, b in zip(x, right(x, zero))]
    y = [a + b for a, b in zip(v, left(v, x[2]))]
    w = [a + b for a, b in zip(y, right(y, x[0]))]
    return [a + b for a, b in zip(w, left(w, x[2] + y[2]))]


def features_kernel(
    counts_ref, x_hbm, f_hbm, g_ref,
    xs, su, sd, hu, hd, fs, tb, gs, pk, r1, r2, ag,
    x_sem, f_sem, su_sem, sd_sem, hu_sem, hd_sem, ex_send, ex_recv,
):
    line, track = lax.axis_index("line"), lax.axis_index("track")
    y, core = line // 2, line % 2
    xx, z = track // 4, track % 4
    chip = 16 * xx + 4 * y + z
    sibling = (2 * y + 1 - core, track)

    def peer(d):
        px, py, pz = (xx + d // 16) % 4, (y + (d // 4) % 4) % 4, (z + d % 4) % 4
        return 16 * px + 4 * py + pz, (2 * py + core, 4 * px + pz)

    crow = 256 * CHUNK

    def load(j):
        n = crow if j < CHUNKS - 1 else ROWS * BANDS - crow * (CHUNKS - 1)
        return pltpu.make_async_copy(
            x_hbm.at[pl.ds(crow * j, n)], xs.at[pl.ds(16 + crow * j, n)], x_sem.at[j]
        )

    for j in range(CHUNKS):
        load(j).start()

    barrier = pltpu.get_barrier_semaphore()
    pl.semaphore_signal(barrier, inc=1, device_id=sibling, device_id_type=MESH)

    def greet(d, carry):
        pl.semaphore_signal(barrier, inc=1, device_id=peer(d)[1], device_id_type=MESH)
        return carry

    lax.fori_loop(1, 64, greet, 0)

    xs[0:16, :] = jnp.zeros((16, COLS), BF16)
    tail = ROWS * (BANDS + 1)
    xs[tail : ROWS * (BP + 2), :] = jnp.zeros((ROWS * (BP + 2) - tail, COLS), BF16)
    for h in (hu, hd):
        h[0:16, :] = jnp.zeros((16, COLS), BF16)
        h[HR - 16 : HR, :] = jnp.zeros((16, COLS), BF16)
    gs[:, 384:512] = jnp.zeros((BP, 128), F32)

    cnt = counts_ref[0, 0]
    ri, ci = iotas((64, 256))
    want = jnp.where(ri < 32, ri & 1, 14 + (ri & 1))
    sel = ((((ri & 31) >> 1) == (ci >> 4)) & (want == (ci & 15)) & (want < cnt)).astype(F32).astype(BF16)

    ri, ci = iotas((128, 160))
    r, b, bi, rr = ri >> 3, ri & 7, ci >> 4, ci & 15
    sign = (bi == b + 2).astype(F32) - (bi == b).astype(F32)
    wt = jnp.where((r < cnt) & (rr < cnt), BIN(jnp.abs(rr - r)), 0.0)
    body = (sign * wt * (1.0 / 512.0)).astype(BF16)

    ri, ci = iotas((64, 128))
    q, b = ri >> 4, ri & 15
    r = jnp.where(q < 2, q, q + 12)
    up = ci < 64
    cj = ci & 63
    bi, rr = cj >> 1, jnp.where(up, (cj & 1) - 2, (cj & 1) + 16)
    sign = (bi == b + 9).astype(F32) - (bi == b + 7).astype(F32)
    have = jnp.where(up, track, TILES - 1 - track) > 0
    wt = jnp.where((r < cnt) & have, BIN(jnp.abs(rr - r)), 0.0)
    rim = (sign * wt * (1.0 / 512.0)).astype(BF16)

    def halo(j):
        rows = pl.ds(pl.multiple_of(16 + 32 * CHUNK * j, 32 * CHUNK // 6), 32 * CHUNK)
        first = pltpu.make_async_remote_copy(
            src_ref=su.at[rows], dst_ref=hd.at[rows], send_sem=su_sem.at[j], recv_sem=hd_sem.at[j],
            device_id=(line, (track + TILES - 1) % TILES), device_id_type=MESH,
        )
        last = pltpu.make_async_remote_copy(
            src_ref=sd.at[rows], dst_ref=hu.at[rows], send_sem=sd_sem.at[j], recv_sem=hu_sem.at[j],
            device_id=(line, (track + 1) % TILES), device_id_type=MESH,
        )
        return first, last

    for j in range(CHUNKS):
        load(j).wait()
        for g in range(CHUNK * j, CHUNK * j + CHUNK):
            picked = jnp.dot(sel, xs[16 + 256 * g : 272 + 256 * g, :], preferred_element_type=F32).astype(BF16)
            su[16 + 32 * g : 48 + 32 * g, :] = picked[0:32]
            sd[16 + 32 * g : 48 + 32 * g, :] = picked[32:64]
        if j == 0:
            pl.semaphore_wait(barrier, 64)
        for copy in halo(j):
            copy.start()

    def interior(g):
        at = pl.multiple_of(16 * g, 16)
        halves = []
        for h in range(2):
            xk = xs[pl.ds(pl.multiple_of(256 * g + 128 * h, 128), 160), :]
            t = jnp.dot(body, xk, preferred_element_type=F32)
            for e, row in enumerate(EDGE):
                tb[e, pl.ds(pl.multiple_of(at + 8 * h, 8), 8), :] = t[8 * row : 8 * row + 8]
            halves.append(smooth_cols(t[16:112]))
        for row in range(2, 14):
            k = 8 * (row - 2)
            for i in range(3):
                both = jnp.concatenate([halves[0][i][k : k + 8], halves[1][i][k : k + 8]], axis=0)
                col = row * COLS + 128 * i
                fs[pl.ds(at, 16), col : col + 128] = both.astype(BF16)

    def interior_step(s, carry):
        for u in range(3):
            interior(3 * s + u)
        return carry

    lax.fori_loop(0, GROUPS // 3, interior_step, 0)

    def outer(lo, hi):
        a = fs[:, lo:hi]
        left = lax.dot_general(a, a[0:256], NT, preferred_element_type=F32)
        right = lax.dot_general(a[256:BP], a[256:BP], NT, preferred_element_type=F32)
        return left, right

    left, right = outer(2 * COLS, 6 * COLS)
    gs[:, 0:256] = left
    gs[256:BP, 256:BP] = right
    for k in (6, 10):
        left, right = outer(k * COLS, (k + 4) * COLS)
        gs[:, 0:256] += left
        gs[256:BP, 256:BP] += right

    def edge(g):
        at = pl.multiple_of(16 * g, 16)
        src = pl.ds(pl.multiple_of(32 * g, 32), 64)
        halos = jnp.concatenate([hu[src, :], hd[src, :]], axis=0)
        t = jnp.dot(rim, halos, preferred_element_type=F32) + tb[:, pl.ds(at, 16), :].reshape(64, COLS)
        out = smooth_cols(t)
        for e, row in enumerate(EDGE):
            for i in range(3):
                col = row * COLS + 128 * i
                fs[pl.ds(at, 16), col : col + 128] = out[i][16 * e : 16 * e + 16].astype(BF16)

    def edge_step(j, carry):
        for copy in halo(j):
            copy.wait_recv()
        for u in (-1, 0, 1):
            edge(CHUNK * j + u)
        return carry

    for copy in halo(0):
        copy.wait_recv()
    edge(0)
    edge(1)
    lax.fori_loop(1, CHUNKS, edge_step, 0)
    edge(GROUPS - 1)

    f_copy = pltpu.make_async_copy(fs, f_hbm, f_sem)
    f_copy.start()

    for k in (0, 14):
        left, right = outer(k * COLS, (k + 2) * COLS)
        gs[:, 0:256] += left
        gs[256:BP, 256:BP] += right

    for t, (rt, ct) in enumerate(LOWER):
        pk[t] = gs[8 * rt : 8 * rt + 8, 128 * ct : 128 * ct + 128]
    for t in range(len(LOWER), 128):
        pk[t] = jnp.zeros((8, 128), F32)

    mine, other = pl.ds(64 * core, 64), pl.ds(64 * (1 - core), 64)
    pair = pltpu.make_async_remote_copy(
        src_ref=pk.at[other], dst_ref=r1, send_sem=ex_send.at[0], recv_sem=ex_recv.at[0],
        device_id=sibling, device_id_type=MESH,
    )
    pair.start()
    pair.wait_recv()
    pk[mine] += r1[...]

    def scatter(d, carry):
        to, device = peer(d)
        pltpu.make_async_remote_copy(
            src_ref=pk.at[64 * core + to], dst_ref=r2.at[d - 1], send_sem=ex_send.at[1], recv_sem=ex_recv.at[1],
            device_id=device, device_id_type=MESH,
        ).start()
        return carry

    lax.fori_loop(1, 64, scatter, 0)
    pltpu.make_async_copy(r2, r2, ex_recv.at[1]).wait()
    ag[64 * core + chip] = pk[64 * core + chip] + jnp.sum(r2[...], axis=0)

    def gather(d, carry):
        device = peer(d)[1]
        tile = ag.at[64 * core + chip]
        pltpu.make_async_remote_copy(
            src_ref=tile, dst_ref=tile, send_sem=ex_send.at[2], recv_sem=ex_recv.at[2],
            device_id=device, device_id_type=MESH,
        ).start()
        return carry

    lax.fori_loop(1, 64, gather, 0)
    pltpu.make_async_copy(r2, r2, ex_recv.at[2]).wait()
    swap = pltpu.make_async_remote_copy(
        src_ref=ag.at[mine], dst_ref=ag.at[mine], send_sem=ex_send.at[3], recv_sem=ex_recv.at[3],
        device_id=sibling, device_id_type=MESH,
    )
    swap.start()
    swap.wait_recv()
    g_ref[...] = ag[...]

    swap.wait_send()
    pair.wait_send()
    pltpu.make_async_copy(r2, r2, ex_send.at[1]).wait()
    pltpu.make_async_copy(r2, r2, ex_send.at[2]).wait()

    def sent(j, carry):
        for copy in halo(j):
            copy.wait_send()
        return carry

    lax.fori_loop(0, CHUNKS, sent, 0)
    f_copy.wait()


def split3(a):
    hi = a.astype(BF16)
    rest = a - hi.astype(F32)
    mid = rest.astype(BF16)
    low = (rest - mid.astype(F32)).astype(BF16)
    return hi, mid, low


def dot6(a, b, dims):
    n = a.shape[0]
    parts = jnp.concatenate(split3(a), axis=0)
    one = lax.dot_general(parts, b[0], dims, preferred_element_type=F32)
    two = lax.dot_general(parts[: 2 * n], b[1], dims, preferred_element_type=F32)
    three = lax.dot_general(parts[:n], b[2], dims, preferred_element_type=F32)
    return one[:n] + (((one[2 * n :] + two[n:]) + three) + (one[n : 2 * n] + two[:n]))


NN = (((1,), (0,)), ((), ()))


def reciprocal(d):
    return 1.0 / d


def inverse_factor(s):
    ri, ci = iotas((8, 128))
    rows = [s[8 * i : 8 * i + 8] + (ci == ri + 64 + 8 * i).astype(F32) for i in range(8)]
    spread = lambda v, k: jnp.broadcast_to(v[k : k + 1], (8, 128))
    for p in range(8):
        cols = {
            i: [jnp.broadcast_to(rows[i][:, 8 * p + l : 8 * p + l + 1], (8, 128)) for l in range(8)]
            for i in range(p, 8)
        }
        pivots = jnp.ones((8, 128), F32)
        for k in range(8):
            pivot = spread(cols[p][k], k)
            pivots = jnp.where(ri == k, pivot, pivots)
            inv = reciprocal(pivot)
            heads = [spread(cols[p][l], k) * inv for l in range(k + 1, 8)]
            row = spread(rows[p], k) * inv
            for i in range(p, 8):
                if i == p and k == 7:
                    continue
                m = jnp.where(ri > k, cols[i][k], 0.0) if i == p else cols[i][k]
                for l in range(k + 1, 8):
                    cols[i][l] = cols[i][l] - m * heads[l - k - 1]
                rows[i] = rows[i] - m * row
        rows[p] = rows[p] * lax.rsqrt(pivots)
    return jnp.concatenate(rows, axis=0)


def iterate_kernel(g_ref, start_ref, f_hbm, proj_ref, scores_hbm, gf, gh, gm, gl, tt, fs, sc, f_sem, o_sem):
    f_copy = pltpu.make_async_copy(f_hbm, fs, f_sem)
    f_copy.start()

    gf[BP:512, :] = jnp.zeros((512 - BP, 512), F32)
    for t, (rt, ct) in enumerate(LOWER):
        tile = g_ref[t]
        if rt == 53 or ct == 3:
            ri, ci = iotas((8, 128))
            tile = jnp.where((ri + 8 * rt < BANDS) & (ci + 128 * ct < BANDS), tile, 0.0)
        gf[8 * rt : 8 * rt + 8, 128 * ct : 128 * ct + 128] = tile
    for i in range(4):
        for j in range(i):
            gf[128 * j : 128 * j + 128, 128 * i : 128 * i + 128] = gf[
                128 * i : 128 * i + 128, 128 * j : 128 * j + 128
            ].T
    for ref, part in zip((gh, gm, gl), split3(gf[...])):
        ref[...] = part

    tt[:, 384:512] = jnp.zeros((RANK, 128), F32)
    tt[:, 0:BANDS] = start_ref[...]

    zeros = jnp.zeros((RANK, 512), BF16)

    def normaliser(t):
        h, m, l = split3(t)
        rhs = tuple(jnp.concatenate([p, zeros], axis=0) for p in (h, m, l))
        return inverse_factor(dot6(t, rhs, NT))

    def apply(w, t):
        rhs = tuple(jnp.concatenate([zeros, p], axis=0) for p in split3(t))
        return dot6(w, rhs, NN)

    def step(i, carry):
        t = tt[...]
        z = dot6(t, (gh[...], gm[...], gl[...]), NN)
        tt[...] = apply(normaliser(t), z)
        return carry

    lax.fori_loop(0, ITERS, step, 0)
    t = tt[...]
    basis = apply(normaliser(t), t)

    h, m, l = split3(basis)
    lhs = jnp.concatenate([h, h, m, m], axis=0).astype(F32).T.astype(BF16)
    rhs = jnp.concatenate([h, m, h, m], axis=0)
    proj = jnp.dot(lhs, rhs, preferred_element_type=F32)
    proj_ref[...] = proj[0:BANDS, 0:BANDS]

    f_copy.wait()
    narrow = h[:, 0:BP]

    def score(r, carry):
        cols = pl.ds(pl.multiple_of(r * COLS, 128), COLS)
        s = jnp.dot(narrow, fs[:, cols], preferred_element_type=F32)
        for i in range(3):
            sc[pl.ds(RANK * ROWS * i + r, RANK, stride=ROWS), :] = s[:, 128 * i : 128 * i + 128]
        return carry

    lax.fori_loop(0, ROWS, score, 0)
    out = [
        pltpu.make_async_copy(
            sc.at[pl.ds(RANK * ROWS * i, RANK * ROWS)], scores_hbm.at[:, pl.ds(128 * i, 128)], o_sem.at[i]
        )
        for i in range(3)
    ]
    for copy in out:
        copy.start()
    for copy in out:
        copy.wait()


def second(tiles, start, features):
    vmem = pl.BlockSpec(memory_space=pltpu.VMEM)
    hbm = pl.BlockSpec(memory_space=pltpu.HBM)
    dma = pltpu.SemaphoreType.DMA
    return pl.pallas_call(
        iterate_kernel,
        out_shape=(
            jax.ShapeDtypeStruct((BANDS, BANDS), F32),
            jax.ShapeDtypeStruct((RANK * ROWS, COLS), F32),
        ),
        in_specs=[vmem, vmem, hbm],
        out_specs=(vmem, hbm),
        scratch_shapes=[
            pltpu.VMEM((512, 512), F32),
            pltpu.VMEM((512, 512), BF16),
            pltpu.VMEM((512, 512), BF16),
            pltpu.VMEM((512, 512), BF16),
            pltpu.VMEM((RANK, 512), F32),
            pltpu.VMEM((BP, ROWS * COLS), BF16),
            pltpu.VMEM((3 * RANK * ROWS, 128), F32),
            dma,
            dma((3,)),
        ],
        compiler_params=pltpu.CompilerParams(vmem_limit_bytes=56 * 2**20),
    )(tiles, start.T, features)


def on_device(radiance, counts, start):
    x = radiance.reshape(BANDS * ROWS, COLS)
    vmem = pl.BlockSpec(memory_space=pltpu.VMEM)
    hbm = pl.BlockSpec(memory_space=pltpu.HBM)
    dma = pltpu.SemaphoreType.DMA
    features, tiles = pl.pallas_call(
        features_kernel,
        out_shape=(
            jax.ShapeDtypeStruct((BP, ROWS * COLS), BF16),
            jax.ShapeDtypeStruct((128, 8, 128), F32),
        ),
        in_specs=[pl.BlockSpec(memory_space=pltpu.SMEM), hbm],
        out_specs=(hbm, vmem),
        scratch_shapes=[
            pltpu.VMEM((ROWS * (BP + 2), COLS), BF16),
            pltpu.VMEM((HR, COLS), BF16),
            pltpu.VMEM((HR, COLS), BF16),
            pltpu.VMEM((HR, COLS), BF16),
            pltpu.VMEM((HR, COLS), BF16),
            pltpu.VMEM((BP, ROWS * COLS), BF16),
            pltpu.VMEM((4, BP, COLS), F32),
            pltpu.VMEM((BP, 512), F32),
            pltpu.VMEM((128, 8, 128), F32),
            pltpu.VMEM((64, 8, 128), F32),
            pltpu.VMEM((63, 8, 128), F32),
            pltpu.VMEM((128, 8, 128), F32),
            dma((CHUNKS,)),
            dma,
            dma((CHUNKS,)),
            dma((CHUNKS,)),
            dma((CHUNKS,)),
            dma((CHUNKS,)),
            dma((4,)),
            dma((4,)),
        ],
        compiler_params=pltpu.CompilerParams(
            collective_id=0, has_side_effects=True, vmem_limit_bytes=56 * 2**20
        ),
    )(counts, x)
    projector, scores = second(tiles, start, features)
    return projector, scores.reshape(1, RANK, ROWS, COLS)


def solution(mesh):
    return jax.shard_map(
        on_device,
        mesh=mesh,
        in_specs=(P("line", None, "track", None), P("line", "track"), P()),
        out_specs=(P(), P("line", None, "track", None)),
        check_vma=False,
    )
```

```python
import functools

import jax
import jax.numpy as jnp
from jax import lax
from jax.experimental import pallas as pl
from jax.experimental.pallas import tpu as pltpu
from jax.sharding import PartitionSpec as P

MESH = pl.DeviceIdType.MESH
F32 = jnp.float32
BF16 = jnp.bfloat16

BANDS = 425
BP = 432
GROUPS = BP // 16
RANK = 64
ITERS = 6
ROWS = 16
COLS = 384
TILES = 16
CHUNK = 3
CHUNKS = GROUPS // CHUNK
HR = 16 + 2 * BP + 16
EDGE = (0, 1, 14, 15)
BIN = lambda dist: jnp.where(dist == 0, 6.0, jnp.where(dist == 1, 4.0, jnp.where(dist == 2, 1.0, 0.0)))
NT = (((1,), (1,)), ((), ()))
LOWER = [(rt, ct) for ct in range(4) for rt in range(16 * ct, BP // 8)]


def iotas(shape):
    return lax.broadcasted_iota(jnp.int32, shape, 0), lax.broadcasted_iota(jnp.int32, shape, 1)


def banded(rows, cols, shift):
    ri, ci = iotas((rows, cols))
    return BIN(jnp.abs(ri + shift - ci)).astype(BF16)


def split2(t, hi_ref, lo_ref, rows):
    hi = t.astype(BF16)
    hi_ref[rows, :] = hi
    lo_ref[rows, :] = (t - hi.astype(F32)).astype(BF16)


def smooth_cols(hi_ref, lo_ref, wl_ref, wr_ref, rows):
    hi, lo = hi_ref[0:rows, :], lo_ref[0:rows, :]
    left = jnp.concatenate([hi[:, 0:256], lo[:, 0:256], hi[:, 256:384], lo[:, 256:384]], axis=1)
    right = jnp.concatenate([hi[:, 128:384], lo[:, 128:384]], axis=1)
    return (
        jnp.dot(left, wl_ref[...], preferred_element_type=F32),
        jnp.dot(right, wr_ref[...], preferred_element_type=F32),
    )


def features_kernel(
    counts_ref, x_hbm, f_hbm, g_ref,
    xs, su, sd, hu, hd, fs, th, tl, wl, wr, tb, gs, pk, r1, r2, ag,
    x_sem, f_sem, su_sem, sd_sem, hu_sem, hd_sem, ex_send, ex_recv, line_sem,
):
    line, track = lax.axis_index("line"), lax.axis_index("track")
    y, core = line // 2, line % 2
    xx, z = track // 4, track % 4
    sibling = (2 * y + 1 - core, track)

    here = (xx, y, z)
    near = [[lax.rem(base + step, 4) for step in range(4)] for base in here]

    def peer(*steps):
        px, py, pz = (near[i][steps[i]] for i in range(3))
        return 16 * px + 4 * py + pz, (2 * py + core, 4 * px + pz)

    on_axis = [[peer(*[step if i == axis else 0 for i in range(3)])[1] for step in (1, 2, 3)] for axis in range(3)]
    others = [(i, j, k) for i in range(4) for j in range(4) for k in range(4)][1:]
    others.sort(key=lambda steps: -sum(min(v, 4 - v) for v in steps))

    before, after = (line, lax.rem(track + TILES - 1, TILES)), (line, lax.rem(track + 1, TILES))
    greeted = [sibling, before, after] + on_axis[0] + on_axis[1] + on_axis[2]

    crow = 256 * CHUNK

    def load(j):
        n = crow if j < CHUNKS - 1 else ROWS * BANDS - crow * (CHUNKS - 1)
        return pltpu.make_async_copy(
            x_hbm.at[pl.ds(crow * j, n)], xs.at[pl.ds(16 + crow * j, n)], x_sem.at[j]
        )

    for j in range(CHUNKS):
        load(j).start()

    barrier = pltpu.get_barrier_semaphore()
    for device in greeted:
        pl.semaphore_signal(barrier, inc=1, device_id=device, device_id_type=MESH)

    xs[0:16, :] = jnp.zeros((16, COLS), BF16)
    tail = ROWS * (BANDS + 1)
    xs[tail : ROWS * (BP + 2), :] = jnp.zeros((ROWS * (BP + 2) - tail, COLS), BF16)
    for h in (hu, hd):
        h[0:16, :] = jnp.zeros((16, COLS), BF16)
        h[HR - 16 : HR, :] = jnp.zeros((16, COLS), BF16)

    cnt = counts_ref[0, 0]
    ri, ci = iotas((64, 256))
    want = jnp.where(ri < 32, ri & 1, 14 + (ri & 1))
    sel = ((((ri & 31) >> 1) == (ci >> 4)) & (want == (ci & 15)) & (want < cnt)).astype(F32).astype(BF16)

    def halo(j):
        rows = pl.ds(pl.multiple_of(16 + 32 * CHUNK * j, 32 * CHUNK // 6), 32 * CHUNK)
        first = pltpu.make_async_remote_copy(
            src_ref=su.at[rows], dst_ref=hd.at[rows], send_sem=su_sem.at[j], recv_sem=hd_sem.at[j],
            device_id=before, device_id_type=MESH,
        )
        last = pltpu.make_async_remote_copy(
            src_ref=sd.at[rows], dst_ref=hu.at[rows], send_sem=sd_sem.at[j], recv_sem=hu_sem.at[j],
            device_id=after, device_id_type=MESH,
        )
        return first, last

    for j in range(CHUNKS):
        load(j).wait()
        for g in range(CHUNK * j, CHUNK * j + CHUNK):
            picked = jnp.dot(sel, xs[16 + 256 * g : 272 + 256 * g, :], preferred_element_type=F32).astype(BF16)
            su[16 + 32 * g : 48 + 32 * g, :] = picked[0:32]
            sd[16 + 32 * g : 48 + 32 * g, :] = picked[32:64]
        if j == 0:
            pl.semaphore_wait(barrier, len(greeted))
            for device in on_axis[1]:
                pl.semaphore_signal(line_sem.at[0], inc=1, device_id=device, device_id_type=MESH)
        for copy in halo(j):
            copy.start()

    ri, ci = iotas((128, 160))
    r, b, bi, rr = ri >> 3, ri & 7, ci >> 4, ci & 15
    sign = (bi == b + 2).astype(F32) - (bi == b).astype(F32)
    wt = jnp.where((r < cnt) & (rr < cnt), BIN(jnp.abs(rr - r)), 0.0)
    body = (sign * wt * (1.0 / 512.0)).astype(BF16)

    ri, ci = iotas((64, 128))
    q, b = ri >> 4, ri & 15
    r = jnp.where(q < 2, q, q + 12)
    up = ci < 64
    cj = ci & 63
    bi, rr = cj >> 1, jnp.where(up, (cj & 1) - 2, (cj & 1) + 16)
    sign = (bi == b + 9).astype(F32) - (bi == b + 7).astype(F32)
    have = jnp.where(up, track, TILES - 1 - track) > 0
    wt = jnp.where((r < cnt) & have, BIN(jnp.abs(rr - r)), 0.0)
    rim = (sign * wt * (1.0 / 512.0)).astype(BF16)

    wl[0:256, :] = banded(256, 256, 0)
    wl[256:512, :] = banded(256, 256, 0)
    wl[512:640, :] = banded(128, 256, 256)
    wl[640:768, :] = banded(128, 256, 256)
    wr[0:256, :] = banded(256, 128, -128)
    wr[256:512, :] = banded(256, 128, -128)

    gs[:, 384:512] = jnp.zeros((BP, 128), F32)

    def interior_step(s, carry):
        for u in range(2 * CHUNK):
            at = pl.multiple_of(16 * CHUNK * s + 8 * u, 8)
            xk = xs[pl.ds(pl.multiple_of(256 * CHUNK * s + 128 * u, 128), 160), :]
            t = jnp.dot(body, xk, preferred_element_type=F32)
            for e, row in enumerate(EDGE):
                tb[e, pl.ds(at, 8), :] = t[8 * row : 8 * row + 8]
            split2(t[16:112], th, tl, slice(96 * u, 96 * u + 96))
        wide = smooth_cols(th, tl, wl, wr, 192 * CHUNK)
        for u in range(CHUNK):
            at = pl.ds(pl.multiple_of(16 * CHUNK * s + 16 * u, 16), 16)
            for row in range(2, 14):
                k = 192 * u + 8 * (row - 2)
                for part, col in zip(wide, (row * COLS, row * COLS + 256)):
                    both = jnp.concatenate([part[k : k + 8], part[k + 96 : k + 104]], axis=0)
                    fs[at, col : col + part.shape[1]] = both.astype(BF16)
        return carry

    lax.fori_loop(0, CHUNKS, interior_step, 0)

    pl.semaphore_wait(line_sem.at[0], 3)
    for device in on_axis[2]:
        pl.semaphore_signal(line_sem.at[1], inc=1, device_id=device, device_id_type=MESH)

    def outer(lo, hi):
        a = fs[:, lo:hi]
        left = lax.dot_general(a, a[0:256], NT, preferred_element_type=F32)
        right = lax.dot_general(a[256:BP], a[256:BP], NT, preferred_element_type=F32)
        return left, right

    left, right = outer(2 * COLS, 6 * COLS)
    gs[:, 0:256] = left
    gs[256:BP, 256:BP] = right
    for k in (6, 10):
        left, right = outer(k * COLS, (k + 4) * COLS)
        gs[:, 0:256] += left
        gs[256:BP, 256:BP] += right

    def edges(first, count):
        for u in range(count):
            at = pl.multiple_of(16 * (first + u), 16)
            src = pl.ds(pl.multiple_of(32 * (first + u), 32), 64)
            halos = jnp.concatenate([hu[src, :], hd[src, :]], axis=0)
            t = jnp.dot(rim, halos, preferred_element_type=F32) + tb[:, pl.ds(at, 16), :].reshape(64, COLS)
            split2(t, th, tl, slice(64 * u, 64 * u + 64))
        wide = smooth_cols(th, tl, wl, wr, 64 * count)
        for u in range(count):
            at = pl.ds(pl.multiple_of(16 * (first + u), 16), 16)
            for e, row in enumerate(EDGE):
                k = 64 * u + 16 * e
                for part, col in zip(wide, (row * COLS, row * COLS + 256)):
                    fs[at, col : col + part.shape[1]] = part[k : k + 16].astype(BF16)

    def edge_step(j, carry):
        for copy in halo(j):
            copy.wait_recv()
        edges(CHUNK * j - 1, CHUNK)
        return carry

    for copy in halo(0):
        copy.wait_recv()
    edges(0, CHUNK - 1)
    lax.fori_loop(1, CHUNKS, edge_step, 0)
    edges(GROUPS - 1, 1)

    f_copy = pltpu.make_async_copy(fs, f_hbm, f_sem)
    f_copy.start()

    for k in (0, 14):
        left, right = outer(k * COLS, (k + 2) * COLS)
        gs[:, 0:256] += left
        gs[256:BP, 256:BP] += right

    for t, (rt, ct) in enumerate(LOWER):
        pk[t] = gs[8 * rt : 8 * rt + 8, 128 * ct : 128 * ct + 128]
    for t in range(len(LOWER), 128):
        pk[t] = jnp.zeros((8, 128), F32)

    def send(phase, src, dst, device):
        pltpu.make_async_remote_copy(
            src_ref=src, dst_ref=dst, send_sem=ex_send.at[phase], recv_sem=ex_recv.at[phase],
            device_id=device, device_id_type=MESH,
        ).start()

    def arrived(phase, ref):
        pltpu.make_async_copy(ref, ref, ex_recv.at[phase]).wait()

    half = pl.ds(64 * core, 64)
    mine = 64 * core + 16 * xx + 4 * y + z
    send(0, pk.at[pl.ds(64 * (1 - core), 64)], r1, sibling)
    pl.semaphore_wait(line_sem.at[1], 3)
    arrived(0, r1)
    pk[half] += r1[...]
    for n, steps in enumerate(others):
        chip, device = peer(*steps)
        send(1, pk.at[64 * core + chip], r2.at[n], device)
    arrived(1, r2)
    ag[mine] = pk[mine] + jnp.sum(r2[...], axis=0)
    for steps in others:
        send(2, ag.at[mine], ag.at[mine], peer(*steps)[1])
    arrived(2, r2)
    send(3, ag.at[half], ag.at[half], sibling)
    arrived(3, r1)
    g_ref[...] = ag[...]

    for phase, ref in enumerate((r1, r2, r2, r1)):
        pltpu.make_async_copy(ref, ref, ex_send.at[phase]).wait()

    def sent(j, carry):
        for copy in halo(j):
            copy.wait_send()
        return carry

    lax.fori_loop(0, CHUNKS, sent, 0)
    f_copy.wait()


def split3(a):
    hi = a.astype(BF16)
    rest = a - hi.astype(F32)
    mid = rest.astype(BF16)
    low = (rest - mid.astype(F32)).astype(BF16)
    return hi, mid, low


def dot6(a, b, dims):
    n = a.shape[0]
    parts = jnp.concatenate(split3(a), axis=0)
    one = lax.dot_general(parts, b[0], dims, preferred_element_type=F32)
    two = lax.dot_general(parts[: 2 * n], b[1], dims, preferred_element_type=F32)
    three = lax.dot_general(parts[:n], b[2], dims, preferred_element_type=F32)
    return one[:n] + (((one[2 * n :] + two[n:]) + three) + (one[n : 2 * n] + two[:n]))


NN = (((1,), (0,)), ((), ()))


def reciprocal(d):
    return 1.0 / d


def inverse_factor(s):
    ri, ci = iotas((8, 128))
    rows = [s[8 * i : 8 * i + 8] + (ci == ri + 64 + 8 * i).astype(F32) for i in range(8)]
    spread = lambda v, k: jnp.broadcast_to(v[k : k + 1], (8, 128))
    for p in range(8):
        cols = {
            i: [jnp.broadcast_to(rows[i][:, 8 * p + l : 8 * p + l + 1], (8, 128)) for l in range(8)]
            for i in range(p, 8)
        }
        pivots = jnp.ones((8, 128), F32)
        for k in range(8):
            pivot = spread(cols[p][k], k)
            pivots = jnp.where(ri == k, pivot, pivots)
            inv = reciprocal(pivot)
            heads = [spread(cols[p][l], k) * inv for l in range(k + 1, 8)]
            row = spread(rows[p], k) * inv
            for i in range(p, 8):
                if i == p and k == 7:
                    continue
                m = jnp.where(ri > k, cols[i][k], 0.0) if i == p else cols[i][k]
                for l in range(k + 1, 8):
                    cols[i][l] = cols[i][l] - m * heads[l - k - 1]
                rows[i] = rows[i] - m * row
        rows[p] = rows[p] * lax.rsqrt(pivots)
    return jnp.concatenate(rows, axis=0)


def iterate_kernel(g_ref, start_ref, f_hbm, proj_ref, scores_hbm, gf, gh, gm, gl, tt, fs, sc, f_sem, o_sem):
    f_copy = pltpu.make_async_copy(f_hbm, fs, f_sem)
    f_copy.start()

    gf[BP:512, :] = jnp.zeros((512 - BP, 512), F32)
    for t, (rt, ct) in enumerate(LOWER):
        tile = g_ref[t]
        if rt == 53 or ct == 3:
            ri, ci = iotas((8, 128))
            tile = jnp.where((ri + 8 * rt < BANDS) & (ci + 128 * ct < BANDS), tile, 0.0)
        gf[8 * rt : 8 * rt + 8, 128 * ct : 128 * ct + 128] = tile
    for i in range(4):
        for j in range(i):
            gf[128 * j : 128 * j + 128, 128 * i : 128 * i + 128] = gf[
                128 * i : 128 * i + 128, 128 * j : 128 * j + 128
            ].T
    for ref, part in zip((gh, gm, gl), split3(gf[...])):
        ref[...] = part

    tt[:, 384:512] = jnp.zeros((RANK, 128), F32)
    tt[:, 0:BANDS] = start_ref[...]

    zeros = jnp.zeros((RANK, 512), BF16)

    def normaliser(t):
        h, m, l = split3(t)
        rhs = tuple(jnp.concatenate([p, zeros], axis=0) for p in (h, m, l))
        return inverse_factor(dot6(t, rhs, NT))

    def apply(w, t):
        rhs = tuple(jnp.concatenate([zeros, p], axis=0) for p in split3(t))
        return dot6(w, rhs, NN)

    def step(i, carry):
        t = tt[...]
        z = dot6(t, (gh[...], gm[...], gl[...]), NN)
        tt[...] = apply(normaliser(t), z)
        return carry

    lax.fori_loop(0, ITERS, step, 0)
    t = tt[...]
    basis = apply(normaliser(t), t)

    h, m, l = split3(basis)
    lhs = jnp.concatenate([h, h, m, m], axis=0).astype(F32).T.astype(BF16)
    rhs = jnp.concatenate([h, m, h, m], axis=0)
    proj = jnp.dot(lhs, rhs, preferred_element_type=F32)
    proj_ref[...] = proj[0:BANDS, 0:BANDS]

    f_copy.wait()
    narrow = h[:, 0:BP]

    def score(r, carry):
        cols = pl.ds(pl.multiple_of(r * COLS, 128), COLS)
        s = jnp.dot(narrow, fs[:, cols], preferred_element_type=F32)
        for i in range(3):
            sc[pl.ds(RANK * ROWS * i + r, RANK, stride=ROWS), :] = s[:, 128 * i : 128 * i + 128]
        return carry

    lax.fori_loop(0, ROWS, score, 0)
    out = [
        pltpu.make_async_copy(
            sc.at[pl.ds(RANK * ROWS * i, RANK * ROWS)], scores_hbm.at[:, pl.ds(128 * i, 128)], o_sem.at[i]
        )
        for i in range(3)
    ]
    for copy in out:
        copy.start()
    for copy in out:
        copy.wait()


def second(tiles, start, features):
    vmem = pl.BlockSpec(memory_space=pltpu.VMEM)
    hbm = pl.BlockSpec(memory_space=pltpu.HBM)
    dma = pltpu.SemaphoreType.DMA
    return pl.pallas_call(
        iterate_kernel,
        out_shape=(
            jax.ShapeDtypeStruct((BANDS, BANDS), F32),
            jax.ShapeDtypeStruct((RANK * ROWS, COLS), F32),
        ),
        in_specs=[vmem, vmem, hbm],
        out_specs=(vmem, hbm),
        scratch_shapes=[
            pltpu.VMEM((512, 512), F32),
            pltpu.VMEM((512, 512), BF16),
            pltpu.VMEM((512, 512), BF16),
            pltpu.VMEM((512, 512), BF16),
            pltpu.VMEM((RANK, 512), F32),
            pltpu.VMEM((BP, ROWS * COLS), BF16),
            pltpu.VMEM((3 * RANK * ROWS, 128), F32),
            dma,
            dma((3,)),
        ],
        compiler_params=pltpu.CompilerParams(vmem_limit_bytes=56 * 2**20),
    )(tiles, start.T, features)


def first(counts, x):
    vmem = pl.BlockSpec(memory_space=pltpu.VMEM)
    hbm = pl.BlockSpec(memory_space=pltpu.HBM)
    dma = pltpu.SemaphoreType.DMA
    return pl.pallas_call(
        features_kernel,
        out_shape=(
            jax.ShapeDtypeStruct((BP, ROWS * COLS), BF16),
            jax.ShapeDtypeStruct((128, 8, 128), F32),
        ),
        in_specs=[pl.BlockSpec(memory_space=pltpu.SMEM), hbm],
        out_specs=(hbm, vmem),
        scratch_shapes=[
            pltpu.VMEM((ROWS * (BP + 2), COLS), BF16),
            pltpu.VMEM((HR, COLS), BF16),
            pltpu.VMEM((HR, COLS), BF16),
            pltpu.VMEM((HR, COLS), BF16),
            pltpu.VMEM((HR, COLS), BF16),
            pltpu.VMEM((BP, ROWS * COLS), BF16),
            pltpu.VMEM((192 * CHUNK, COLS), BF16),
            pltpu.VMEM((192 * CHUNK, COLS), BF16),
            pltpu.VMEM((768, 256), BF16),
            pltpu.VMEM((512, 128), BF16),
            pltpu.VMEM((4, BP, COLS), F32),
            pltpu.VMEM((BP, 512), F32),
            pltpu.VMEM((128, 8, 128), F32),
            pltpu.VMEM((64, 8, 128), F32),
            pltpu.VMEM((63, 8, 128), F32),
            pltpu.VMEM((128, 8, 128), F32),
            dma((CHUNKS,)),
            dma,
            dma((CHUNKS,)),
            dma((CHUNKS,)),
            dma((CHUNKS,)),
            dma((CHUNKS,)),
            dma((4,)),
            dma((4,)),
            pltpu.SemaphoreType.REGULAR((2,)),
        ],
        compiler_params=pltpu.CompilerParams(
            collective_id=0, has_side_effects=True, vmem_limit_bytes=56 * 2**20
        ),
    )(counts, x)


def on_device(radiance, counts, start):
    x = radiance.reshape(BANDS * ROWS, COLS)
    features, tiles = first(counts, x)
    projector, scores = second(tiles, start, features)
    return projector, scores.reshape(1, RANK, ROWS, COLS)


def solution(mesh):
    return jax.shard_map(
        on_device,
        mesh=mesh,
        in_specs=(P("line", None, "track", None), P("line", "track"), P()),
        out_specs=(P(), P("line", None, "track", None)),
        check_vma=False,
    )
```

```python
import functools

import jax
import jax.numpy as jnp
from jax import lax
from jax.experimental import pallas as pl
from jax.experimental.pallas import tpu as pltpu
from jax.sharding import PartitionSpec as P

MESH = pl.DeviceIdType.MESH
F32 = jnp.float32
BF16 = jnp.bfloat16

BANDS = 425
BP = 432
GROUPS = BP // 16
RANK = 64
ITERS = 6
ROWS = 16
COLS = 384
TILES = 16
CHUNK = 3
CHUNKS = GROUPS // CHUNK
HR = 16 + 2 * BP + 16
EDGE = (0, 1, 14, 15)
BIN = lambda dist: jnp.where(dist == 0, 6.0, jnp.where(dist == 1, 4.0, jnp.where(dist == 2, 1.0, 0.0)))
NT = (((1,), (1,)), ((), ()))
LOWER = [(rt, ct) for ct in range(4) for rt in range(16 * ct, BP // 8)]


def iotas(shape):
    return lax.broadcasted_iota(jnp.int32, shape, 0), lax.broadcasted_iota(jnp.int32, shape, 1)


def banded(rows, cols, shift):
    ri, ci = iotas((rows, cols))
    return BIN(jnp.abs(ri + shift - ci)).astype(BF16)


def split2(t, hi_ref, lo_ref, rows):
    hi = t.astype(BF16)
    hi_ref[rows, :] = hi
    lo_ref[rows, :] = (t - hi.astype(F32)).astype(BF16)


def smooth_cols(hi_ref, lo_ref, wl_ref, wr_ref, rows):
    hi, lo = hi_ref[0:rows, :], lo_ref[0:rows, :]
    left = jnp.concatenate([hi[:, 0:256], lo[:, 0:256], hi[:, 256:384], lo[:, 256:384]], axis=1)
    right = jnp.concatenate([hi[:, 128:384], lo[:, 128:384]], axis=1)
    return (
        jnp.dot(left, wl_ref[...], preferred_element_type=F32),
        jnp.dot(right, wr_ref[...], preferred_element_type=F32),
    )


def split3(a):
    hi = a.astype(BF16)
    rest = a - hi.astype(F32)
    mid = rest.astype(BF16)
    low = (rest - mid.astype(F32)).astype(BF16)
    return hi, mid, low


def dot6(a, b, dims):
    n = a.shape[0]
    parts = jnp.concatenate(split3(a), axis=0)
    one = lax.dot_general(parts, b[0], dims, preferred_element_type=F32)
    two = lax.dot_general(parts[: 2 * n], b[1], dims, preferred_element_type=F32)
    three = lax.dot_general(parts[:n], b[2], dims, preferred_element_type=F32)
    return one[:n] + (((one[2 * n :] + two[n:]) + three) + (one[n : 2 * n] + two[:n]))


NN = (((1,), (0,)), ((), ()))


def inverse_factor(s):
    ri, ci = iotas((8, 128))
    spread = lambda v, k: jnp.broadcast_to(v[k : k + 1], (8, 128))
    rows = [s[8 * i : 8 * i + 8] + (ci == ri + 64 + 8 * i).astype(F32) for i in range(8)]

    def columns(p, i):
        return [jnp.broadcast_to(rows[i][:, 8 * p + l : 8 * p + l + 1], (8, 128)) for l in range(8)]

    ahead = columns(0, 0)
    for p in range(8):
        pivots = jnp.ones((8, 128), F32)
        cols, steps = ahead + (columns(p + 1, p) if p < 7 else []), []
        width = len(cols)
        for k in range(8):
            pivot = spread(cols[k], k)
            pivots = jnp.where(ri == k, pivot, pivots)
            inv = 1.0 / pivot
            heads = [spread(cols[l], k) * inv for l in range(k + 1, width)]
            row = spread(rows[p], k) * inv
            steps.append((heads, row))
            if k < 7:
                m = jnp.where(ri > k, cols[k], 0.0)
                for l in range(k + 1, width):
                    cols[l] = cols[l] - m * heads[l - k - 1]
                rows[p] = rows[p] - m * row
        for i in range(p + 1, 8):
            cols = columns(p, i) + (columns(p + 1, i) if i == p + 1 else [])
            for k, (heads, row) in enumerate(steps):
                for l in range(k + 1, len(cols)):
                    cols[l] = cols[l] - cols[k] * heads[l - k - 1]
                rows[i] = rows[i] - cols[k] * row
            if i == p + 1:
                ahead = cols[8:]
        rows[p] = rows[p] * lax.rsqrt(pivots)
    return jnp.concatenate(rows, axis=0)


def normaliser(t):
    zeros = jnp.zeros((RANK, 512), BF16)
    return inverse_factor(dot6(t, tuple(jnp.concatenate([p, zeros], axis=0) for p in split3(t)), NT))


def apply(w, t):
    zeros = jnp.zeros((RANK, 512), BF16)
    return dot6(w, tuple(jnp.concatenate([zeros, p], axis=0) for p in split3(t)), NN)


def features_kernel(
    counts_ref, x_hbm, start_hbm, f_hbm, g_ref, b_ref,
    xs, su, sd, hu, hd, fs, th, tl, wl, wr, tb, gs, pk, r1, r2, ag, st,
    x_sem, f_sem, su_sem, sd_sem, hu_sem, hd_sem, ex_send, ex_recv, line_sem, st_sem,
):
    line, track = lax.axis_index("line"), lax.axis_index("track")
    y, core = line // 2, line % 2
    xx, z = track // 4, track % 4
    sibling = (2 * y + 1 - core, track)

    here = (xx, y, z)
    near = [[lax.rem(base + step, 4) for step in range(4)] for base in here]

    def peer(*steps):
        px, py, pz = (near[i][steps[i]] for i in range(3))
        return 16 * px + 4 * py + pz, (2 * py + core, 4 * px + pz)

    on_axis = [[peer(*[step if i == axis else 0 for i in range(3)])[1] for step in (1, 2, 3)] for axis in range(3)]
    others = [(i, j, k) for i in range(4) for j in range(4) for k in range(4)][1:]
    others.sort(key=lambda steps: -sum(min(v, 4 - v) for v in steps))

    before, after = (line, lax.rem(track + TILES - 1, TILES)), (line, lax.rem(track + 1, TILES))
    greeted = [sibling, before, after] + on_axis[0] + on_axis[1] + on_axis[2]

    crow = 256 * CHUNK

    def load(j):
        n = crow if j < CHUNKS - 1 else ROWS * BANDS - crow * (CHUNKS - 1)
        return pltpu.make_async_copy(
            x_hbm.at[pl.ds(crow * j, n)], xs.at[pl.ds(16 + crow * j, n)], x_sem.at[j]
        )

    for j in range(CHUNKS):
        load(j).start()
    st_copy = pltpu.make_async_copy(start_hbm, st, st_sem)
    st_copy.start()

    barrier = pltpu.get_barrier_semaphore()
    for device in greeted:
        pl.semaphore_signal(barrier, inc=1, device_id=device, device_id_type=MESH)

    xs[0:16, :] = jnp.zeros((16, COLS), BF16)
    tail = ROWS * (BANDS + 1)
    xs[tail : ROWS * (BP + 2), :] = jnp.zeros((ROWS * (BP + 2) - tail, COLS), BF16)
    for h in (hu, hd):
        h[0:16, :] = jnp.zeros((16, COLS), BF16)
        h[HR - 16 : HR, :] = jnp.zeros((16, COLS), BF16)

    cnt = counts_ref[0, 0]
    ri, ci = iotas((64, 256))
    want = jnp.where(ri < 32, ri & 1, 14 + (ri & 1))
    sel = ((((ri & 31) >> 1) == (ci >> 4)) & (want == (ci & 15)) & (want < cnt)).astype(F32).astype(BF16)

    def halo(j):
        rows = pl.ds(pl.multiple_of(16 + 32 * CHUNK * j, 32 * CHUNK // 6), 32 * CHUNK)
        first = pltpu.make_async_remote_copy(
            src_ref=su.at[rows], dst_ref=hd.at[rows], send_sem=su_sem.at[j], recv_sem=hd_sem.at[j],
            device_id=before, device_id_type=MESH,
        )
        last = pltpu.make_async_remote_copy(
            src_ref=sd.at[rows], dst_ref=hu.at[rows], send_sem=sd_sem.at[j], recv_sem=hu_sem.at[j],
            device_id=after, device_id_type=MESH,
        )
        return first, last

    for j in range(CHUNKS):
        load(j).wait()
        for g in range(CHUNK * j, CHUNK * j + CHUNK):
            picked = jnp.dot(sel, xs[16 + 256 * g : 272 + 256 * g, :], preferred_element_type=F32).astype(BF16)
            su[16 + 32 * g : 48 + 32 * g, :] = picked[0:32]
            sd[16 + 32 * g : 48 + 32 * g, :] = picked[32:64]
        if j == 0:
            pl.semaphore_wait(barrier, len(greeted))
            for device in on_axis[1]:
                pl.semaphore_signal(line_sem.at[0], inc=1, device_id=device, device_id_type=MESH)
        for copy in halo(j):
            copy.start()

    ri, ci = iotas((128, 160))
    r, b, bi, rr = ri >> 3, ri & 7, ci >> 4, ci & 15
    sign = (bi == b + 2).astype(F32) - (bi == b).astype(F32)
    wt = jnp.where((r < cnt) & (rr < cnt), BIN(jnp.abs(rr - r)), 0.0)
    body = (sign * wt * (1.0 / 512.0)).astype(BF16)

    ri, ci = iotas((64, 128))
    q, b = ri >> 4, ri & 15
    r = jnp.where(q < 2, q, q + 12)
    up = ci < 64
    cj = ci & 63
    bi, rr = cj >> 1, jnp.where(up, (cj & 1) - 2, (cj & 1) + 16)
    sign = (bi == b + 9).astype(F32) - (bi == b + 7).astype(F32)
    have = jnp.where(up, track, TILES - 1 - track) > 0
    wt = jnp.where((r < cnt) & have, BIN(jnp.abs(rr - r)), 0.0)
    rim = (sign * wt * (1.0 / 512.0)).astype(BF16)

    wl[0:256, :] = banded(256, 256, 0)
    wl[256:512, :] = banded(256, 256, 0)
    wl[512:640, :] = banded(128, 256, 256)
    wl[640:768, :] = banded(128, 256, 256)
    wr[0:256, :] = banded(256, 128, -128)
    wr[256:512, :] = banded(256, 128, -128)

    gs[:, 384:512] = jnp.zeros((BP, 128), F32)

    def interior_step(s, carry):
        for u in range(2 * CHUNK):
            at = pl.multiple_of(16 * CHUNK * s + 8 * u, 8)
            xk = xs[pl.ds(pl.multiple_of(256 * CHUNK * s + 128 * u, 128), 160), :]
            t = jnp.dot(body, xk, preferred_element_type=F32)
            for e, row in enumerate(EDGE):
                tb[e, pl.ds(at, 8), :] = t[8 * row : 8 * row + 8]
            split2(t[16:112], th, tl, slice(96 * u, 96 * u + 96))
        wide = smooth_cols(th, tl, wl, wr, 192 * CHUNK)
        for u in range(CHUNK):
            at = pl.ds(pl.multiple_of(16 * CHUNK * s + 16 * u, 16), 16)
            for row in range(2, 14):
                k = 192 * u + 8 * (row - 2)
                for part, col in zip(wide, (row * COLS, row * COLS + 256)):
                    both = jnp.concatenate([part[k : k + 8], part[k + 96 : k + 104]], axis=0)
                    fs[at, col : col + part.shape[1]] = both.astype(BF16)
        return carry

    lax.fori_loop(0, CHUNKS, interior_step, 0)

    pl.semaphore_wait(line_sem.at[0], 3)
    for device in on_axis[2]:
        pl.semaphore_signal(line_sem.at[1], inc=1, device_id=device, device_id_type=MESH)

    def outer(lo, hi):
        a = fs[:, lo:hi]
        left = lax.dot_general(a, a[0:256], NT, preferred_element_type=F32)
        right = lax.dot_general(a[256:BP], a[256:BP], NT, preferred_element_type=F32)
        return left, right

    left, right = outer(2 * COLS, 6 * COLS)
    gs[:, 0:256] = left
    gs[256:BP, 256:BP] = right
    for k in (6, 10):
        left, right = outer(k * COLS, (k + 4) * COLS)
        gs[:, 0:256] += left
        gs[256:BP, 256:BP] += right

    def edges(first, count):
        for u in range(count):
            at = pl.multiple_of(16 * (first + u), 16)
            src = pl.ds(pl.multiple_of(32 * (first + u), 32), 64)
            halos = jnp.concatenate([hu[src, :], hd[src, :]], axis=0)
            t = jnp.dot(rim, halos, preferred_element_type=F32) + tb[:, pl.ds(at, 16), :].reshape(64, COLS)
            split2(t, th, tl, slice(64 * u, 64 * u + 64))
        wide = smooth_cols(th, tl, wl, wr, 64 * count)
        for u in range(count):
            at = pl.ds(pl.multiple_of(16 * (first + u), 16), 16)
            for e, row in enumerate(EDGE):
                k = 64 * u + 16 * e
                for part, col in zip(wide, (row * COLS, row * COLS + 256)):
                    fs[at, col : col + part.shape[1]] = part[k : k + 16].astype(BF16)

    def edge_step(j, carry):
        for copy in halo(j):
            copy.wait_recv()
        edges(CHUNK * j - 1, CHUNK)
        return carry

    for copy in halo(0):
        copy.wait_recv()
    edges(0, CHUNK - 1)
    lax.fori_loop(1, CHUNKS - 1, edge_step, 0)
    for copy in halo(CHUNKS - 1):
        copy.wait_recv()
    edges(GROUPS - CHUNK - 1, CHUNK + 1)

    f_copy = pltpu.make_async_copy(fs, f_hbm, f_sem)
    f_copy.start()

    for k in (0, 14):
        left, right = outer(k * COLS, (k + 2) * COLS)
        gs[:, 0:256] += left
        gs[256:BP, 256:BP] += right

    for t, (rt, ct) in enumerate(LOWER):
        pk[t] = gs[8 * rt : 8 * rt + 8, 128 * ct : 128 * ct + 128]
    for t in range(len(LOWER), 128):
        pk[t] = jnp.zeros((8, 128), F32)

    def send(phase, src, dst, device):
        pltpu.make_async_remote_copy(
            src_ref=src, dst_ref=dst, send_sem=ex_send.at[phase], recv_sem=ex_recv.at[phase],
            device_id=device, device_id_type=MESH,
        ).start()

    def arrived(phase, ref):
        pltpu.make_async_copy(ref, ref, ex_recv.at[phase]).wait()

    half = pl.ds(64 * core, 64)
    mine = 64 * core + 16 * xx + 4 * y + z
    send(0, pk.at[pl.ds(64 * (1 - core), 64)], r1, sibling)
    pl.semaphore_wait(line_sem.at[1], 3)
    arrived(0, r1)
    pk[half] += r1[...]
    for n, steps in enumerate(others):
        chip, device = peer(*steps)
        send(1, pk.at[64 * core + chip], r2.at[n], device)
    st_copy.wait()
    begin = jnp.concatenate([st[...], jnp.zeros((RANK, 512 - BANDS), F32)], axis=1)
    b_ref[...] = apply(normaliser(begin), begin)
    arrived(1, r2)
    ag[mine] = pk[mine] + jnp.sum(r2[...], axis=0)
    for steps in others:
        send(2, ag.at[mine], ag.at[mine], peer(*steps)[1])
    arrived(2, r2)
    send(3, ag.at[half], ag.at[half], sibling)
    arrived(3, r1)
    g_ref[...] = ag[...]

    for phase, ref in enumerate((r1, r2, r2, r1)):
        pltpu.make_async_copy(ref, ref, ex_send.at[phase]).wait()

    def sent(j, carry):
        for copy in halo(j):
            copy.wait_send()
        return carry

    lax.fori_loop(0, CHUNKS, sent, 0)
    f_copy.wait()


def iterate_kernel(g_ref, first_ref, f_hbm, proj_ref, scores_hbm, gf, gh, gm, gl, tt, fs, sc, f_sem, o_sem):
    f_copy = pltpu.make_async_copy(f_hbm, fs, f_sem)
    f_copy.start()

    gf[BP:512, :] = jnp.zeros((512 - BP, 512), F32)
    for t, (rt, ct) in enumerate(LOWER):
        tile = g_ref[t]
        if rt == 53 or ct == 3:
            ri, ci = iotas((8, 128))
            tile = jnp.where((ri + 8 * rt < BANDS) & (ci + 128 * ct < BANDS), tile, 0.0)
        gf[8 * rt : 8 * rt + 8, 128 * ct : 128 * ct + 128] = tile
    for i in range(4):
        for j in range(i):
            gf[128 * j : 128 * j + 128, 128 * i : 128 * i + 128] = gf[
                128 * i : 128 * i + 128, 128 * j : 128 * j + 128
            ].T
    for ref, part in zip((gh, gm, gl), split3(gf[...])):
        ref[...] = part

    tt[...] = dot6(first_ref[...], (gh[...], gm[...], gl[...]), NN)

    def step(i, carry):
        t = tt[...]
        z = dot6(t, (gh[...], gm[...], gl[...]), NN)
        tt[...] = apply(normaliser(t), z)
        return carry

    lax.fori_loop(1, ITERS, step, 0)
    t = tt[...]
    basis = apply(normaliser(t), t)

    h, m, l = split3(basis)
    lhs = jnp.concatenate([h, h, m, m], axis=0).astype(F32).T.astype(BF16)
    rhs = jnp.concatenate([h, m, h, m], axis=0)
    proj = jnp.dot(lhs, rhs, preferred_element_type=F32)
    proj_ref[...] = proj[0:BANDS, 0:BANDS]

    f_copy.wait()
    narrow = h[:, 0:BP]

    out = [
        pltpu.make_async_copy(
            sc.at[pl.ds(RANK * ROWS * i, RANK * ROWS)], scores_hbm.at[:, pl.ds(128 * i, 128)], o_sem.at[i]
        )
        for i in range(3)
    ]
    for i in range(3):
        for r in range(ROWS):
            col = r * COLS + 128 * i
            part = jnp.dot(narrow, fs[:, col : col + 128], preferred_element_type=F32)
            sc[pl.ds(RANK * ROWS * i + r, RANK, stride=ROWS), :] = part
        out[i].start()
    for copy in out:
        copy.wait()


def second(tiles, begin, features):
    vmem = pl.BlockSpec(memory_space=pltpu.VMEM)
    hbm = pl.BlockSpec(memory_space=pltpu.HBM)
    dma = pltpu.SemaphoreType.DMA
    return pl.pallas_call(
        iterate_kernel,
        out_shape=(
            jax.ShapeDtypeStruct((BANDS, BANDS), F32),
            jax.ShapeDtypeStruct((RANK * ROWS, COLS), F32),
        ),
        in_specs=[vmem, vmem, hbm],
        out_specs=(vmem, hbm),
        scratch_shapes=[
            pltpu.VMEM((512, 512), F32),
            pltpu.VMEM((512, 512), BF16),
            pltpu.VMEM((512, 512), BF16),
            pltpu.VMEM((512, 512), BF16),
            pltpu.VMEM((RANK, 512), F32),
            pltpu.VMEM((BP, ROWS * COLS), BF16),
            pltpu.VMEM((3 * RANK * ROWS, 128), F32),
            dma,
            dma((3,)),
        ],
        compiler_params=pltpu.CompilerParams(vmem_limit_bytes=53 * 2**20),
    )(tiles, begin, features)


def first(counts, x, start):
    vmem = pl.BlockSpec(memory_space=pltpu.VMEM)
    hbm = pl.BlockSpec(memory_space=pltpu.HBM)
    dma = pltpu.SemaphoreType.DMA
    return pl.pallas_call(
        features_kernel,
        out_shape=(
            jax.ShapeDtypeStruct((BP, ROWS * COLS), BF16),
            jax.ShapeDtypeStruct((128, 8, 128), F32),
            jax.ShapeDtypeStruct((RANK, 512), F32),
        ),
        in_specs=[pl.BlockSpec(memory_space=pltpu.SMEM), hbm, hbm],
        out_specs=(hbm, vmem, vmem),
        scratch_shapes=[
            pltpu.VMEM((ROWS * (BP + 2), COLS), BF16),
            pltpu.VMEM((HR, COLS), BF16),
            pltpu.VMEM((HR, COLS), BF16),
            pltpu.VMEM((HR, COLS), BF16),
            pltpu.VMEM((HR, COLS), BF16),
            pltpu.VMEM((BP, ROWS * COLS), BF16),
            pltpu.VMEM((192 * CHUNK, COLS), BF16),
            pltpu.VMEM((192 * CHUNK, COLS), BF16),
            pltpu.VMEM((768, 256), BF16),
            pltpu.VMEM((512, 128), BF16),
            pltpu.VMEM((4, BP, COLS), F32),
            pltpu.VMEM((BP, 512), F32),
            pltpu.VMEM((128, 8, 128), F32),
            pltpu.VMEM((64, 8, 128), F32),
            pltpu.VMEM((63, 8, 128), F32),
            pltpu.VMEM((128, 8, 128), F32),
            pltpu.VMEM((RANK, BANDS), F32),
            dma((CHUNKS,)),
            dma,
            dma((CHUNKS,)),
            dma((CHUNKS,)),
            dma((CHUNKS,)),
            dma((CHUNKS,)),
            dma((4,)),
            dma((4,)),
            pltpu.SemaphoreType.REGULAR((2,)),
            dma,
        ],
        compiler_params=pltpu.CompilerParams(
            collective_id=0, has_side_effects=True, vmem_limit_bytes=53 * 2**20
        ),
    )(counts, x, start.T)


def on_device(radiance, counts, start):
    x = radiance.reshape(BANDS * ROWS, COLS)
    features, tiles, begin = first(counts, x, start)
    projector, scores = second(tiles, begin, features)
    return projector, scores.reshape(1, RANK, ROWS, COLS)


def solution(mesh):
    return jax.shard_map(
        on_device,
        mesh=mesh,
        in_specs=(P("line", None, "track", None), P("line", "track"), P()),
        out_specs=(P(), P("line", None, "track", None)),
        check_vma=False,
    )
```

```python
import functools

import jax
import jax.numpy as jnp
from jax import lax
from jax.experimental import pallas as pl
from jax.experimental.pallas import tpu as pltpu
from jax.sharding import PartitionSpec as P

MESH = pl.DeviceIdType.MESH
F32 = jnp.float32
BF16 = jnp.bfloat16

BANDS = 425
BP = 432
GROUPS = BP // 16
RANK = 64
ITERS = 6
ROWS = 16
COLS = 384
TILES = 16
CHUNK = 3
CHUNKS = GROUPS // CHUNK
SENT = [CHUNK] * (CHUNKS - 1) + [CHUNK - 1, 1]
HR = 16 + 2 * BP + 16
EDGE = (0, 1, 14, 15)
BIN = lambda dist: jnp.where(dist == 0, 6.0, jnp.where(dist == 1, 4.0, jnp.where(dist == 2, 1.0, 0.0)))
NT = (((1,), (1,)), ((), ()))
LOWER = [(rt, ct) for ct in range(4) for rt in range(16 * ct, BP // 8)]


def iotas(shape):
    return lax.broadcasted_iota(jnp.int32, shape, 0), lax.broadcasted_iota(jnp.int32, shape, 1)


def banded(rows, cols, shift):
    ri, ci = iotas((rows, cols))
    return BIN(jnp.abs(ri + shift - ci)).astype(BF16)


def split2(t, hi_ref, lo_ref, rows):
    hi = t.astype(BF16)
    hi_ref[rows, :] = hi
    lo_ref[rows, :] = (t - hi.astype(F32)).astype(BF16)


def smooth_cols(hi_ref, lo_ref, wl_ref, wr_ref, rows):
    hi, lo = hi_ref[0:rows, :], lo_ref[0:rows, :]
    left = jnp.concatenate([hi[:, 0:256], lo[:, 0:256], hi[:, 256:384], lo[:, 256:384]], axis=1)
    right = jnp.concatenate([hi[:, 128:384], lo[:, 128:384]], axis=1)
    return (
        jnp.dot(left, wl_ref[...], preferred_element_type=F32),
        jnp.dot(right, wr_ref[...], preferred_element_type=F32),
    )


def split3(a):
    hi = a.astype(BF16)
    rest = a - hi.astype(F32)
    mid = rest.astype(BF16)
    low = (rest - mid.astype(F32)).astype(BF16)
    return hi, mid, low


def dot6(a, b, dims):
    n = a.shape[0]
    parts = jnp.concatenate(split3(a), axis=0)
    one = lax.dot_general(parts, b[0], dims, preferred_element_type=F32)
    two = lax.dot_general(parts[: 2 * n], b[1], dims, preferred_element_type=F32)
    three = lax.dot_general(parts[:n], b[2], dims, preferred_element_type=F32)
    return one[:n] + (((one[2 * n :] + two[n:]) + three) + (one[n : 2 * n] + two[:n]))


NN = (((1,), (0,)), ((), ()))


def inverse_factor(s):
    ri, ci = iotas((8, 128))
    spread = lambda v, k: jnp.broadcast_to(v[k : k + 1], (8, 128))
    rows = [s[8 * i : 8 * i + 8] + (ci == ri + 64 + 8 * i).astype(F32) for i in range(8)]

    def columns(p, i):
        return [jnp.broadcast_to(rows[i][:, 8 * p + l : 8 * p + l + 1], (8, 128)) for l in range(8)]

    ahead = columns(0, 0)
    for p in range(8):
        pivots = jnp.ones((8, 128), F32)
        cols, steps = ahead + (columns(p + 1, p) if p < 7 else []), []
        width = len(cols)
        for k in range(8):
            pivot = spread(cols[k], k)
            pivots = jnp.where(ri == k, pivot, pivots)
            inv = 1.0 / pivot
            heads = [spread(cols[l], k) * inv for l in range(k + 1, width)]
            row = spread(rows[p], k) * inv
            steps.append((heads, row))
            if k < 7:
                m = jnp.where(ri > k, cols[k], 0.0)
                for l in range(k + 1, width):
                    cols[l] = cols[l] - m * heads[l - k - 1]
                rows[p] = rows[p] - m * row
        for i in range(p + 1, 8):
            cols = columns(p, i) + (columns(p + 1, i) if i == p + 1 else [])
            for k, (heads, row) in enumerate(steps):
                for l in range(k + 1, len(cols)):
                    cols[l] = cols[l] - cols[k] * heads[l - k - 1]
                rows[i] = rows[i] - cols[k] * row
            if i == p + 1:
                ahead = cols[8:]
        rows[p] = rows[p] * lax.rsqrt(pivots)
    return jnp.concatenate(rows, axis=0)


def normaliser(t):
    zeros = jnp.zeros((RANK, 512), BF16)
    return inverse_factor(dot6(t, tuple(jnp.concatenate([p, zeros], axis=0) for p in split3(t)), NT))


def apply(w, t):
    zeros = jnp.zeros((RANK, 512), BF16)
    return dot6(w, tuple(jnp.concatenate([zeros, p], axis=0) for p in split3(t)), NN)


def features_kernel(
    counts_ref, x_hbm, start_hbm, f_hbm, g_ref, b_ref,
    xs, su, sd, hu, hd, fs, th, tl, wl, wr, tb, gs, pk, r1, r2, ag, st,
    x_sem, f_sem, su_sem, sd_sem, hu_sem, hd_sem, ex_send, ex_recv, line_sem, st_sem,
):
    line, track = lax.axis_index("line"), lax.axis_index("track")
    y, core = line // 2, line % 2
    xx, z = track // 4, track % 4
    sibling = (2 * y + 1 - core, track)

    here = (xx, y, z)
    near = [[lax.rem(base + step, 4) for step in range(4)] for base in here]

    def peer(*steps):
        px, py, pz = (near[i][steps[i]] for i in range(3))
        return 16 * px + 4 * py + pz, (2 * py + core, 4 * px + pz)

    on_axis = [[peer(*[step if i == axis else 0 for i in range(3)])[1] for step in (1, 2, 3)] for axis in range(3)]
    others = [(i, j, k) for i in range(4) for j in range(4) for k in range(4)][1:]
    others.sort(key=lambda steps: -sum(min(v, 4 - v) for v in steps))

    before, after = (line, lax.rem(track + TILES - 1, TILES)), (line, lax.rem(track + 1, TILES))
    greeted = [sibling, before, after] + on_axis[0] + on_axis[1] + on_axis[2]

    crow = 256 * CHUNK

    def load(j):
        n = crow if j < CHUNKS - 1 else ROWS * BANDS - crow * (CHUNKS - 1)
        return pltpu.make_async_copy(
            x_hbm.at[pl.ds(crow * j, n)], xs.at[pl.ds(16 + crow * j, n)], x_sem.at[j]
        )

    for j in range(CHUNKS):
        load(j).start()
    st_copy = pltpu.make_async_copy(start_hbm, st, st_sem)
    st_copy.start()

    barrier = pltpu.get_barrier_semaphore()
    for device in greeted:
        pl.semaphore_signal(barrier, inc=1, device_id=device, device_id_type=MESH)

    xs[0:16, :] = jnp.zeros((16, COLS), BF16)
    tail = ROWS * (BANDS + 1)
    xs[tail : ROWS * (BP + 2), :] = jnp.zeros((ROWS * (BP + 2) - tail, COLS), BF16)
    for h in (hu, hd):
        h[0:16, :] = jnp.zeros((16, COLS), BF16)
        h[HR - 16 : HR, :] = jnp.zeros((16, COLS), BF16)

    cnt = counts_ref[0, 0]
    ri, ci = iotas((64, 256))
    want = jnp.where(ri < 32, ri & 1, 14 + (ri & 1))
    sel = ((((ri & 31) >> 1) == (ci >> 4)) & (want == (ci & 15)) & (want < cnt)).astype(F32).astype(BF16)

    def halo(j):
        if isinstance(j, int):
            rows = pl.ds(16 + 32 * sum(SENT[:j]), 32 * SENT[j])
        else:
            rows = pl.ds(pl.multiple_of(16 + 32 * CHUNK * j, 16), 32 * CHUNK)
        first = pltpu.make_async_remote_copy(
            src_ref=su.at[rows], dst_ref=hd.at[rows], send_sem=su_sem.at[j], recv_sem=hd_sem.at[j],
            device_id=before, device_id_type=MESH,
        )
        last = pltpu.make_async_remote_copy(
            src_ref=sd.at[rows], dst_ref=hu.at[rows], send_sem=sd_sem.at[j], recv_sem=hu_sem.at[j],
            device_id=after, device_id_type=MESH,
        )
        return first, last

    for j in range(len(SENT)):
        if j < CHUNKS:
            load(j).wait()
        for g in range(sum(SENT[:j]), sum(SENT[: j + 1])):
            picked = jnp.dot(sel, xs[16 + 256 * g : 272 + 256 * g, :], preferred_element_type=F32).astype(BF16)
            su[16 + 32 * g : 48 + 32 * g, :] = picked[0:32]
            sd[16 + 32 * g : 48 + 32 * g, :] = picked[32:64]
        if j == 0:
            pl.semaphore_wait(barrier, len(greeted))
            for device in on_axis[1]:
                pl.semaphore_signal(line_sem.at[0], inc=1, device_id=device, device_id_type=MESH)
        for copy in halo(j):
            copy.start()

    ri, ci = iotas((128, 160))
    r, b, bi, rr = ri >> 3, ri & 7, ci >> 4, ci & 15
    sign = (bi == b + 2).astype(F32) - (bi == b).astype(F32)
    wt = jnp.where((r < cnt) & (rr < cnt), BIN(jnp.abs(rr - r)), 0.0)
    body = (sign * wt * (1.0 / 512.0)).astype(BF16)

    ri, ci = iotas((64, 128))
    q, b = ri >> 4, ri & 15
    r = jnp.where(q < 2, q, q + 12)
    up = ci < 64
    cj = ci & 63
    bi, rr = cj >> 1, jnp.where(up, (cj & 1) - 2, (cj & 1) + 16)
    sign = (bi == b + 9).astype(F32) - (bi == b + 7).astype(F32)
    have = jnp.where(up, track, TILES - 1 - track) > 0
    wt = jnp.where((r < cnt) & have, BIN(jnp.abs(rr - r)), 0.0)
    rim = (sign * wt * (1.0 / 512.0)).astype(BF16)

    wl[0:256, :] = banded(256, 256, 0)
    wl[256:512, :] = banded(256, 256, 0)
    wl[512:640, :] = banded(128, 256, 256)
    wl[640:768, :] = banded(128, 256, 256)
    wr[0:256, :] = banded(256, 128, -128)
    wr[256:512, :] = banded(256, 128, -128)

    gs[:, 384:512] = jnp.zeros((BP, 128), F32)

    def interior_step(s, carry):
        for u in range(2 * CHUNK):
            at = pl.multiple_of(16 * CHUNK * s + 8 * u, 8)
            xk = xs[pl.ds(pl.multiple_of(256 * CHUNK * s + 128 * u, 128), 160), :]
            t = jnp.dot(body, xk, preferred_element_type=F32)
            for e, row in enumerate(EDGE):
                tb[e, pl.ds(at, 8), :] = t[8 * row : 8 * row + 8]
            split2(t[16:112], th, tl, slice(96 * u, 96 * u + 96))
        wide = smooth_cols(th, tl, wl, wr, 192 * CHUNK)
        for u in range(CHUNK):
            at = pl.ds(pl.multiple_of(16 * CHUNK * s + 16 * u, 16), 16)
            for row in range(2, 14):
                k = 192 * u + 8 * (row - 2)
                for part, col in zip(wide, (row * COLS, row * COLS + 256)):
                    both = jnp.concatenate([part[k : k + 8], part[k + 96 : k + 104]], axis=0)
                    fs[at, col : col + part.shape[1]] = both.astype(BF16)
        return carry

    lax.fori_loop(0, CHUNKS, interior_step, 0)

    pl.semaphore_wait(line_sem.at[0], 3)
    for device in on_axis[2]:
        pl.semaphore_signal(line_sem.at[1], inc=1, device_id=device, device_id_type=MESH)

    def outer(lo, hi):
        a = fs[:, lo:hi]
        left = lax.dot_general(a, a[0:256], NT, preferred_element_type=F32)
        right = lax.dot_general(a[256:BP], a[256:BP], NT, preferred_element_type=F32)
        return left, right

    left, right = outer(2 * COLS, 6 * COLS)
    gs[:, 0:256] = left
    gs[256:BP, 256:BP] = right
    for k in (6, 10):
        left, right = outer(k * COLS, (k + 4) * COLS)
        gs[:, 0:256] += left
        gs[256:BP, 256:BP] += right

    def edges(first, count):
        for u in range(count):
            at = pl.multiple_of(16 * (first + u), 16)
            src = pl.ds(pl.multiple_of(32 * (first + u), 32), 64)
            halos = jnp.concatenate([hu[src, :], hd[src, :]], axis=0)
            t = jnp.dot(rim, halos, preferred_element_type=F32) + tb[:, pl.ds(at, 16), :].reshape(64, COLS)
            split2(t, th, tl, slice(64 * u, 64 * u + 64))
        wide = smooth_cols(th, tl, wl, wr, 64 * count)
        for u in range(count):
            at = pl.ds(pl.multiple_of(16 * (first + u), 16), 16)
            for e, row in enumerate(EDGE):
                k = 64 * u + 16 * e
                for part, col in zip(wide, (row * COLS, row * COLS + 256)):
                    fs[at, col : col + part.shape[1]] = part[k : k + 16].astype(BF16)

    def edge_step(j, carry):
        for copy in halo(j):
            copy.wait_recv()
        edges(CHUNK * j - 1, CHUNK)
        return carry

    for copy in halo(0):
        copy.wait_recv()
    edges(0, CHUNK - 1)
    lax.fori_loop(1, CHUNKS - 1, edge_step, 0)
    for copy in halo(CHUNKS - 1):
        copy.wait_recv()
    edges(GROUPS - CHUNK - 1, 2)
    for copy in halo(CHUNKS):
        copy.wait_recv()
    edges(GROUPS - 2, 2)

    f_copy = pltpu.make_async_copy(fs, f_hbm, f_sem)
    f_copy.start()

    for k in (0, 14):
        left, right = outer(k * COLS, (k + 2) * COLS)
        gs[:, 0:256] += left
        gs[256:BP, 256:BP] += right

    for t, (rt, ct) in enumerate(LOWER):
        pk[t] = gs[8 * rt : 8 * rt + 8, 128 * ct : 128 * ct + 128]
    for t in range(len(LOWER), 128):
        pk[t] = jnp.zeros((8, 128), F32)

    def send(phase, src, dst, device):
        pltpu.make_async_remote_copy(
            src_ref=src, dst_ref=dst, send_sem=ex_send.at[phase], recv_sem=ex_recv.at[phase],
            device_id=device, device_id_type=MESH,
        ).start()

    def arrived(phase, ref):
        pltpu.make_async_copy(ref, ref, ex_recv.at[phase]).wait()

    half = pl.ds(64 * core, 64)
    mine = 64 * core + 16 * xx + 4 * y + z
    send(0, pk.at[pl.ds(64 * (1 - core), 64)], r1, sibling)
    pl.semaphore_wait(line_sem.at[1], 3)
    arrived(0, r1)
    pk[half] += r1[...]
    for n, steps in enumerate(others):
        chip, device = peer(*steps)
        send(1, pk.at[64 * core + chip], r2.at[n], device)
    st_copy.wait()
    begin = jnp.concatenate([st[...], jnp.zeros((RANK, 512 - BANDS), F32)], axis=1)
    b_ref[...] = apply(normaliser(begin), begin)
    arrived(1, r2)
    ag[mine] = pk[mine] + jnp.sum(r2[...], axis=0)
    for steps in others:
        send(2, ag.at[mine], ag.at[mine], peer(*steps)[1])
    arrived(2, r2)
    send(3, ag.at[half], ag.at[half], sibling)
    arrived(3, r1)
    g_ref[...] = ag[...]

    for phase, ref in enumerate((r1, r2, r2, r1)):
        pltpu.make_async_copy(ref, ref, ex_send.at[phase]).wait()

    def sent(j, carry):
        for copy in halo(j):
            copy.wait_send()
        return carry

    lax.fori_loop(0, CHUNKS - 1, sent, 0)
    for j in (CHUNKS - 1, CHUNKS):
        sent(j, 0)
    f_copy.wait()


def iterate_kernel(g_ref, first_ref, f_hbm, proj_hbm, scores_hbm, gf, gh, gm, gl, tt, fs, sc, pj, f_sem, o_sem, p_sem):
    f_copy = pltpu.make_async_copy(f_hbm, fs, f_sem)
    f_copy.start()

    gf[BP:512, :] = jnp.zeros((512 - BP, 512), F32)
    for t, (rt, ct) in enumerate(LOWER):
        tile = g_ref[t]
        if rt == 53 or ct == 3:
            ri, ci = iotas((8, 128))
            tile = jnp.where((ri + 8 * rt < BANDS) & (ci + 128 * ct < BANDS), tile, 0.0)
        gf[8 * rt : 8 * rt + 8, 128 * ct : 128 * ct + 128] = tile
    for i in range(4):
        for j in range(i):
            gf[128 * j : 128 * j + 128, 128 * i : 128 * i + 128] = gf[
                128 * i : 128 * i + 128, 128 * j : 128 * j + 128
            ].T
    for ref, part in zip((gh, gm, gl), split3(gf[...])):
        ref[...] = part

    tt[...] = dot6(first_ref[...], (gh[...], gm[...], gl[...]), NN)

    def step(i, carry):
        t = tt[...]
        z = dot6(t, (gh[...], gm[...], gl[...]), NN)
        tt[...] = apply(normaliser(t), z)
        return carry

    lax.fori_loop(1, ITERS, step, 0)
    t = tt[...]
    basis = apply(normaliser(t), t)

    h, m, l = split3(basis)
    lhs = jnp.concatenate([h, h, m, m], axis=0).astype(F32).T.astype(BF16)
    rhs = jnp.concatenate([h, m, h, m], axis=0)
    proj = jnp.dot(lhs, rhs, preferred_element_type=F32)
    pj[...] = proj[0:BANDS, 0:BANDS]
    p_copy = pltpu.make_async_copy(pj, proj_hbm, p_sem)
    p_copy.start()

    f_copy.wait()
    narrow = h[:, 0:BP]

    out = [
        pltpu.make_async_copy(
            sc.at[pl.ds(RANK * ROWS * i, RANK * ROWS)], scores_hbm.at[:, pl.ds(128 * i, 128)], o_sem.at[i]
        )
        for i in range(3)
    ]
    for i in range(3):
        for r in range(ROWS):
            col = r * COLS + 128 * i
            part = jnp.dot(narrow, fs[:, col : col + 128], preferred_element_type=F32)
            sc[pl.ds(RANK * ROWS * i + r, RANK, stride=ROWS), :] = part
        out[i].start()
    for copy in out:
        copy.wait()
    p_copy.wait()


def second(tiles, begin, features):
    vmem = pl.BlockSpec(memory_space=pltpu.VMEM)
    hbm = pl.BlockSpec(memory_space=pltpu.HBM)
    dma = pltpu.SemaphoreType.DMA
    return pl.pallas_call(
        iterate_kernel,
        out_shape=(
            jax.ShapeDtypeStruct((BANDS, BANDS), F32),
            jax.ShapeDtypeStruct((RANK * ROWS, COLS), F32),
        ),
        in_specs=[vmem, vmem, hbm],
        out_specs=(hbm, hbm),
        scratch_shapes=[
            pltpu.VMEM((512, 512), F32),
            pltpu.VMEM((512, 512), BF16),
            pltpu.VMEM((512, 512), BF16),
            pltpu.VMEM((512, 512), BF16),
            pltpu.VMEM((RANK, 512), F32),
            pltpu.VMEM((BP, ROWS * COLS), BF16),
            pltpu.VMEM((3 * RANK * ROWS, 128), F32),
            pltpu.VMEM((BANDS, BANDS), F32),
            dma,
            dma((3,)),
            dma,
        ],
        compiler_params=pltpu.CompilerParams(vmem_limit_bytes=53 * 2**20),
    )(tiles, begin, features)


def first(counts, x, start):
    vmem = pl.BlockSpec(memory_space=pltpu.VMEM)
    hbm = pl.BlockSpec(memory_space=pltpu.HBM)
    dma = pltpu.SemaphoreType.DMA
    return pl.pallas_call(
        features_kernel,
        out_shape=(
            jax.ShapeDtypeStruct((BP, ROWS * COLS), BF16),
            jax.ShapeDtypeStruct((128, 8, 128), F32),
            jax.ShapeDtypeStruct((RANK, 512), F32),
        ),
        in_specs=[pl.BlockSpec(memory_space=pltpu.SMEM), hbm, hbm],
        out_specs=(hbm, vmem, vmem),
        scratch_shapes=[
            pltpu.VMEM((ROWS * (BP + 2), COLS), BF16),
            pltpu.VMEM((HR, COLS), BF16),
            pltpu.VMEM((HR, COLS), BF16),
            pltpu.VMEM((HR, COLS), BF16),
            pltpu.VMEM((HR, COLS), BF16),
            pltpu.VMEM((BP, ROWS * COLS), BF16),
            pltpu.VMEM((192 * CHUNK, COLS), BF16),
            pltpu.VMEM((192 * CHUNK, COLS), BF16),
            pltpu.VMEM((768, 256), BF16),
            pltpu.VMEM((512, 128), BF16),
            pltpu.VMEM((4, BP, COLS), F32),
            pltpu.VMEM((BP, 512), F32),
            pltpu.VMEM((128, 8, 128), F32),
            pltpu.VMEM((64, 8, 128), F32),
            pltpu.VMEM((63, 8, 128), F32),
            pltpu.VMEM((128, 8, 128), F32),
            pltpu.VMEM((RANK, BANDS), F32),
            dma((CHUNKS,)),
            dma,
            dma((CHUNKS + 1,)),
            dma((CHUNKS + 1,)),
            dma((CHUNKS + 1,)),
            dma((CHUNKS + 1,)),
            dma((4,)),
            dma((4,)),
            pltpu.SemaphoreType.REGULAR((2,)),
            dma,
        ],
        compiler_params=pltpu.CompilerParams(
            collective_id=0, has_side_effects=True, vmem_limit_bytes=53 * 2**20
        ),
    )(counts, x, start.T)


def on_device(radiance, counts, start):
    x = radiance.reshape(BANDS * ROWS, COLS)
    features, tiles, begin = first(counts, x, start)
    projector, scores = second(tiles, begin, features)
    return projector, scores.reshape(1, RANK, ROWS, COLS)


def solution(mesh):
    return jax.shard_map(
        on_device,
        mesh=mesh,
        in_specs=(P("line", None, "track", None), P("line", "track"), P()),
        out_specs=(P(), P("line", None, "track", None)),
        check_vma=False,
    )
```

```python
import functools

import jax
import jax.numpy as jnp
from jax import lax
from jax.experimental import pallas as pl
from jax.experimental.pallas import tpu as pltpu
from jax.sharding import PartitionSpec as P

MESH = pl.DeviceIdType.MESH
F32 = jnp.float32
BF16 = jnp.bfloat16

BANDS = 425
BP = 432
GROUPS = BP // 16
RANK = 64
ITERS = 6
ROWS = 16
COLS = 384
TILES = 16
CHUNK = 3
CHUNKS = GROUPS // CHUNK
SENT = [CHUNK] * (CHUNKS - 1) + [CHUNK - 1, 1]
HR = 16 + 2 * BP + 16
EDGE = (0, 1, 14, 15)
BIN = lambda dist: jnp.where(dist == 0, 6.0, jnp.where(dist == 1, 4.0, jnp.where(dist == 2, 1.0, 0.0)))
NT = (((1,), (1,)), ((), ()))
LOWER = [(rt, ct) for ct in range(4) for rt in range(16 * ct, BP // 8)]


def iotas(shape):
    return lax.broadcasted_iota(jnp.int32, shape, 0), lax.broadcasted_iota(jnp.int32, shape, 1)


def banded(rows, cols, shift):
    ri, ci = iotas((rows, cols))
    return BIN(jnp.abs(ri + shift - ci)).astype(BF16)


def split2(t, hi_ref, lo_ref, rows):
    hi = t.astype(BF16)
    hi_ref[rows, :] = hi
    lo_ref[rows, :] = (t - hi.astype(F32)).astype(BF16)


def smooth_cols(hi_ref, lo_ref, wl_ref, wr_ref, rows):
    hi, lo = hi_ref[0:rows, :], lo_ref[0:rows, :]
    left = jnp.concatenate([hi[:, 0:256], lo[:, 0:256], hi[:, 256:384], lo[:, 256:384]], axis=1)
    right = jnp.concatenate([hi[:, 128:384], lo[:, 128:384]], axis=1)
    return (
        jnp.dot(left, wl_ref[...], preferred_element_type=F32),
        jnp.dot(right, wr_ref[...], preferred_element_type=F32),
    )


def split3(a):
    hi = a.astype(BF16)
    rest = a - hi.astype(F32)
    mid = rest.astype(BF16)
    low = (rest - mid.astype(F32)).astype(BF16)
    return hi, mid, low


def dot6(a, b, dims):
    n = a.shape[0]
    parts = jnp.concatenate(split3(a), axis=0)
    one = lax.dot_general(parts, b[0], dims, preferred_element_type=F32)
    two = lax.dot_general(parts[: 2 * n], b[1], dims, preferred_element_type=F32)
    three = lax.dot_general(parts[:n], b[2], dims, preferred_element_type=F32)
    return one[:n] + (((one[2 * n :] + two[n:]) + three) + (one[n : 2 * n] + two[:n]))


NN = (((1,), (0,)), ((), ()))


def inverse_factor(s):
    ri, ci = iotas((8, 128))
    spread = lambda v, k: jnp.broadcast_to(v[k : k + 1], (8, 128))
    rows = [s[8 * i : 8 * i + 8] + (ci == ri + 64 + 8 * i).astype(F32) for i in range(8)]

    def columns(p, i):
        return [
            jnp.take_along_axis(rows[i], jnp.full((8, 128), 8 * p + l, jnp.int32), axis=1, mode="promise_in_bounds")
            for l in range(8)
        ]

    ahead = columns(0, 0)
    for p in range(8):
        pivots = jnp.ones((8, 128), F32)
        cols, steps = ahead + (columns(p + 1, p) if p < 7 else []), []
        width = len(cols)
        for k in range(8):
            pivot = spread(cols[k], k)
            pivots = jnp.where(ri == k, pivot, pivots)
            inv = 1.0 / pivot
            heads = [spread(cols[l], k) * inv for l in range(k + 1, width)]
            row = spread(rows[p], k) * inv
            steps.append((heads, row))
            if k < 7:
                m = jnp.where(ri > k, cols[k], 0.0)
                for l in range(k + 1, width):
                    cols[l] = cols[l] - m * heads[l - k - 1]
                rows[p] = rows[p] - m * row
        for i in range(p + 1, 8):
            cols = columns(p, i) + (columns(p + 1, i) if i == p + 1 else [])
            for k, (heads, row) in enumerate(steps):
                for l in range(k + 1, len(cols)):
                    cols[l] = cols[l] - cols[k] * heads[l - k - 1]
                rows[i] = rows[i] - cols[k] * row
            if i == p + 1:
                ahead = cols[8:]
        rows[p] = rows[p] * lax.rsqrt(pivots)
    return jnp.concatenate(rows, axis=0)


def inner(t):
    zeros = jnp.zeros((RANK, 512), BF16)
    return dot6(t, tuple(jnp.concatenate([p, zeros], axis=0) for p in split3(t)), NT)


def apply(w, t):
    zeros = jnp.zeros((RANK, 512), BF16)
    return dot6(w, tuple(jnp.concatenate([zeros, p], axis=0) for p in split3(t)), NN)


def features_kernel(
    counts_ref, x_hbm, start_hbm, f_hbm, g_ref, b_ref,
    xs, su, sd, hu, hd, fs, th, tl, wl, wr, tb, gs, pk, r1, r2, ag, st,
    x_sem, f_sem, su_sem, sd_sem, hu_sem, hd_sem, ex_send, ex_recv, line_sem, st_sem,
):
    line, track = lax.axis_index("line"), lax.axis_index("track")
    y, core = line // 2, line % 2
    xx, z = track // 4, track % 4
    sibling = (2 * y + 1 - core, track)

    here = (xx, y, z)
    near = [[lax.rem(base + step, 4) for step in range(4)] for base in here]

    def peer(*steps):
        px, py, pz = (near[i][steps[i]] for i in range(3))
        return 16 * px + 4 * py + pz, (2 * py + core, 4 * px + pz)

    on_axis = [[peer(*[step if i == axis else 0 for i in range(3)])[1] for step in (1, 2, 3)] for axis in range(3)]
    others = [(i, j, k) for i in range(4) for j in range(4) for k in range(4)][1:]
    others.sort(key=lambda steps: -sum(min(v, 4 - v) for v in steps))

    before, after = (line, lax.rem(track + TILES - 1, TILES)), (line, lax.rem(track + 1, TILES))
    greeted = [sibling, before, after] + on_axis[0] + on_axis[1] + on_axis[2]

    crow = 256 * CHUNK

    def load(j):
        n = crow if j < CHUNKS - 1 else ROWS * BANDS - crow * (CHUNKS - 1)
        return pltpu.make_async_copy(
            x_hbm.at[pl.ds(crow * j, n)], xs.at[pl.ds(16 + crow * j, n)], x_sem.at[j]
        )

    for j in range(CHUNKS):
        load(j).start()
    st_copy = pltpu.make_async_copy(start_hbm, st, st_sem)
    st_copy.start()

    barrier = pltpu.get_barrier_semaphore()
    for device in greeted:
        pl.semaphore_signal(barrier, inc=1, device_id=device, device_id_type=MESH)

    xs[0:16, :] = jnp.zeros((16, COLS), BF16)
    tail = ROWS * (BANDS + 1)
    xs[tail : ROWS * (BP + 2), :] = jnp.zeros((ROWS * (BP + 2) - tail, COLS), BF16)
    for h in (hu, hd):
        h[0:16, :] = jnp.zeros((16, COLS), BF16)
        h[HR - 16 : HR, :] = jnp.zeros((16, COLS), BF16)

    cnt = counts_ref[0, 0]
    ri, ci = iotas((64, 256))
    want = jnp.where(ri < 32, ri & 1, 14 + (ri & 1))
    sel = ((((ri & 31) >> 1) == (ci >> 4)) & (want == (ci & 15)) & (want < cnt)).astype(F32).astype(BF16)

    def halo(j):
        if isinstance(j, int):
            rows = pl.ds(16 + 32 * sum(SENT[:j]), 32 * SENT[j])
        else:
            rows = pl.ds(pl.multiple_of(16 + 32 * CHUNK * j, 16), 32 * CHUNK)
        first = pltpu.make_async_remote_copy(
            src_ref=su.at[rows], dst_ref=hd.at[rows], send_sem=su_sem.at[j], recv_sem=hd_sem.at[j],
            device_id=before, device_id_type=MESH,
        )
        last = pltpu.make_async_remote_copy(
            src_ref=sd.at[rows], dst_ref=hu.at[rows], send_sem=sd_sem.at[j], recv_sem=hu_sem.at[j],
            device_id=after, device_id_type=MESH,
        )
        return first, last

    for j in range(len(SENT)):
        if j < CHUNKS:
            load(j).wait()
        for g in range(sum(SENT[:j]), sum(SENT[: j + 1])):
            picked = jnp.dot(sel, xs[16 + 256 * g : 272 + 256 * g, :], preferred_element_type=F32).astype(BF16)
            su[16 + 32 * g : 48 + 32 * g, :] = picked[0:32]
            sd[16 + 32 * g : 48 + 32 * g, :] = picked[32:64]
        if j == 0:
            pl.semaphore_wait(barrier, len(greeted))
            for device in on_axis[1]:
                pl.semaphore_signal(line_sem.at[0], inc=1, device_id=device, device_id_type=MESH)
        for copy in halo(j):
            copy.start()

    ri, ci = iotas((128, 160))
    r, b, bi, rr = ri >> 3, ri & 7, ci >> 4, ci & 15
    sign = (bi == b + 2).astype(F32) - (bi == b).astype(F32)
    wt = jnp.where((r < cnt) & (rr < cnt), BIN(jnp.abs(rr - r)), 0.0)
    body = (sign * wt * (1.0 / 512.0)).astype(BF16)

    ri, ci = iotas((64, 128))
    q, b = ri >> 4, ri & 15
    r = jnp.where(q < 2, q, q + 12)
    up = ci < 64
    cj = ci & 63
    bi, rr = cj >> 1, jnp.where(up, (cj & 1) - 2, (cj & 1) + 16)
    sign = (bi == b + 9).astype(F32) - (bi == b + 7).astype(F32)
    have = jnp.where(up, track, TILES - 1 - track) > 0
    wt = jnp.where((r < cnt) & have, BIN(jnp.abs(rr - r)), 0.0)
    rim = (sign * wt * (1.0 / 512.0)).astype(BF16)

    wl[0:256, :] = banded(256, 256, 0)
    wl[256:512, :] = banded(256, 256, 0)
    wl[512:640, :] = banded(128, 256, 256)
    wl[640:768, :] = banded(128, 256, 256)
    wr[0:256, :] = banded(256, 128, -128)
    wr[256:512, :] = banded(256, 128, -128)

    gs[:, 384:512] = jnp.zeros((BP, 128), F32)

    def interior_step(s, carry):
        for u in range(2 * CHUNK):
            at = pl.multiple_of(16 * CHUNK * s + 8 * u, 8)
            xk = xs[pl.ds(pl.multiple_of(256 * CHUNK * s + 128 * u, 128), 160), :]
            t = jnp.dot(body, xk, preferred_element_type=F32)
            for e, row in enumerate(EDGE):
                tb[e, pl.ds(at, 8), :] = t[8 * row : 8 * row + 8]
            split2(t[16:112], th, tl, slice(96 * u, 96 * u + 96))
        wide = smooth_cols(th, tl, wl, wr, 192 * CHUNK)
        for u in range(CHUNK):
            at = pl.ds(pl.multiple_of(16 * CHUNK * s + 16 * u, 16), 16)
            for row in range(2, 14):
                k = 192 * u + 8 * (row - 2)
                for part, col in zip(wide, (row * COLS, row * COLS + 256)):
                    both = jnp.concatenate([part[k : k + 8], part[k + 96 : k + 104]], axis=0)
                    fs[at, col : col + part.shape[1]] = both.astype(BF16)
        return carry

    lax.fori_loop(0, CHUNKS, interior_step, 0)

    pl.semaphore_wait(line_sem.at[0], 3)
    for device in on_axis[2]:
        pl.semaphore_signal(line_sem.at[1], inc=1, device_id=device, device_id_type=MESH)

    def outer(lo, hi):
        a = fs[:, lo:hi]
        left = lax.dot_general(a, a[0:256], NT, preferred_element_type=F32)
        right = lax.dot_general(a[256:BP], a[256:BP], NT, preferred_element_type=F32)
        return left, right

    left, right = outer(2 * COLS, 6 * COLS)
    gs[:, 0:256] = left
    gs[256:BP, 256:BP] = right
    for k in (6, 10):
        left, right = outer(k * COLS, (k + 4) * COLS)
        gs[:, 0:256] += left
        gs[256:BP, 256:BP] += right

    def edges(first, count):
        for u in range(count):
            at = pl.multiple_of(16 * (first + u), 16)
            src = pl.ds(pl.multiple_of(32 * (first + u), 32), 64)
            halos = jnp.concatenate([hu[src, :], hd[src, :]], axis=0)
            t = jnp.dot(rim, halos, preferred_element_type=F32) + tb[:, pl.ds(at, 16), :].reshape(64, COLS)
            split2(t, th, tl, slice(64 * u, 64 * u + 64))
        wide = smooth_cols(th, tl, wl, wr, 64 * count)
        for u in range(count):
            at = pl.ds(pl.multiple_of(16 * (first + u), 16), 16)
            for e, row in enumerate(EDGE):
                k = 64 * u + 16 * e
                for part, col in zip(wide, (row * COLS, row * COLS + 256)):
                    fs[at, col : col + part.shape[1]] = part[k : k + 16].astype(BF16)

    def edge_step(j, carry):
        for copy in halo(j):
            copy.wait_recv()
        edges(CHUNK * j - 1, CHUNK)
        return carry

    for copy in halo(0):
        copy.wait_recv()
    edges(0, CHUNK - 1)
    lax.fori_loop(1, CHUNKS - 1, edge_step, 0)
    for copy in halo(CHUNKS - 1):
        copy.wait_recv()
    edges(GROUPS - CHUNK - 1, 2)
    for copy in halo(CHUNKS):
        copy.wait_recv()
    edges(GROUPS - 2, 2)

    f_copy = pltpu.make_async_copy(fs, f_hbm, f_sem)
    f_copy.start()

    for k in (0, 14):
        left, right = outer(k * COLS, (k + 2) * COLS)
        gs[:, 0:256] += left
        gs[256:BP, 256:BP] += right

    for t, (rt, ct) in enumerate(LOWER):
        pk[t] = gs[8 * rt : 8 * rt + 8, 128 * ct : 128 * ct + 128]
    for t in range(len(LOWER), 128):
        pk[t] = jnp.zeros((8, 128), F32)

    def send(phase, src, dst, device):
        pltpu.make_async_remote_copy(
            src_ref=src, dst_ref=dst, send_sem=ex_send.at[phase], recv_sem=ex_recv.at[phase],
            device_id=device, device_id_type=MESH,
        ).start()

    def arrived(phase, ref):
        pltpu.make_async_copy(ref, ref, ex_recv.at[phase]).wait()

    half = pl.ds(64 * core, 64)
    mine = 64 * core + 16 * xx + 4 * y + z
    send(0, pk.at[pl.ds(64 * (1 - core), 64)], r1, sibling)
    pl.semaphore_wait(line_sem.at[1], 3)
    arrived(0, r1)
    pk[half] += r1[...]
    for n, steps in enumerate(others):
        chip, device = peer(*steps)
        send(1, pk.at[64 * core + chip], r2.at[n], device)
    st_copy.wait()
    begin = jnp.concatenate([st[...], jnp.zeros((RANK, 512 - BANDS), F32)], axis=1)
    b_ref[...] = apply(inverse_factor(inner(begin)), begin)
    arrived(1, r2)
    ag[mine] = pk[mine] + jnp.sum(r2[...], axis=0)
    for steps in others:
        send(2, ag.at[mine], ag.at[mine], peer(*steps)[1])
    arrived(2, r2)
    send(3, ag.at[half], ag.at[half], sibling)
    arrived(3, r1)
    g_ref[...] = ag[...]

    for phase, ref in enumerate((r1, r2, r2, r1)):
        pltpu.make_async_copy(ref, ref, ex_send.at[phase]).wait()

    def sent(j, carry):
        for copy in halo(j):
            copy.wait_send()
        return carry

    lax.fori_loop(0, CHUNKS - 1, sent, 0)
    for j in (CHUNKS - 1, CHUNKS):
        sent(j, 0)
    f_copy.wait()


def iterate_kernel(g_ref, first_ref, f_hbm, proj_hbm, scores_hbm, gf, gh, gm, gl, tt, fs, sc, pj, f_sem, o_sem, p_sem):
    f_copy = pltpu.make_async_copy(f_hbm, fs, f_sem)
    f_copy.start()

    gf[BP:512, :] = jnp.zeros((512 - BP, 512), F32)
    for t, (rt, ct) in enumerate(LOWER):
        tile = g_ref[t]
        if rt == 53 or ct == 3:
            ri, ci = iotas((8, 128))
            tile = jnp.where((ri + 8 * rt < BANDS) & (ci + 128 * ct < BANDS), tile, 0.0)
        gf[8 * rt : 8 * rt + 8, 128 * ct : 128 * ct + 128] = tile
    for i in range(4):
        for j in range(i):
            gf[128 * j : 128 * j + 128, 128 * i : 128 * i + 128] = gf[
                128 * i : 128 * i + 128, 128 * j : 128 * j + 128
            ].T
    for ref, part in zip((gh, gm, gl), split3(gf[...])):
        ref[...] = part

    tt[...] = dot6(first_ref[...], (gh[...], gm[...], gl[...]), NN)

    def step(i, carry):
        t = tt[...]
        s = inner(t)
        z = dot6(t, (gh[...], gm[...], gl[...]), NN)
        tt[...] = apply(inverse_factor(s), z)
        return carry

    lax.fori_loop(1, ITERS, step, 0)
    t = tt[...]
    basis = apply(inverse_factor(inner(t)), t)

    h, m, l = split3(basis)
    lhs = jnp.concatenate([h, h, m, m], axis=0).astype(F32).T.astype(BF16)
    rhs = jnp.concatenate([h, m, h, m], axis=0)
    proj = jnp.dot(lhs, rhs, preferred_element_type=F32)
    pj[...] = proj[0:BANDS, 0:BANDS]
    p_copy = pltpu.make_async_copy(pj, proj_hbm, p_sem)
    p_copy.start()

    f_copy.wait()
    narrow = h[:, 0:BP]

    out = [
        pltpu.make_async_copy(
            sc.at[pl.ds(RANK * ROWS * i, RANK * ROWS)], scores_hbm.at[:, pl.ds(128 * i, 128)], o_sem.at[i]
        )
        for i in range(3)
    ]
    for i in range(3):
        for r in range(ROWS):
            col = r * COLS + 128 * i
            part = jnp.dot(narrow, fs[:, col : col + 128], preferred_element_type=F32)
            sc[pl.ds(RANK * ROWS * i + r, RANK, stride=ROWS), :] = part
        out[i].start()
    for copy in out:
        copy.wait()
    p_copy.wait()


def second(tiles, begin, features):
    vmem = pl.BlockSpec(memory_space=pltpu.VMEM)
    hbm = pl.BlockSpec(memory_space=pltpu.HBM)
    dma = pltpu.SemaphoreType.DMA
    return pl.pallas_call(
        iterate_kernel,
        out_shape=(
            jax.ShapeDtypeStruct((BANDS, BANDS), F32),
            jax.ShapeDtypeStruct((RANK * ROWS, COLS), F32),
        ),
        in_specs=[vmem, vmem, hbm],
        out_specs=(hbm, hbm),
        scratch_shapes=[
            pltpu.VMEM((512, 512), F32),
            pltpu.VMEM((512, 512), BF16),
            pltpu.VMEM((512, 512), BF16),
            pltpu.VMEM((512, 512), BF16),
            pltpu.VMEM((RANK, 512), F32),
            pltpu.VMEM((BP, ROWS * COLS), BF16),
            pltpu.VMEM((3 * RANK * ROWS, 128), F32),
            pltpu.VMEM((BANDS, BANDS), F32),
            dma,
            dma((3,)),
            dma,
        ],
        compiler_params=pltpu.CompilerParams(vmem_limit_bytes=53 * 2**20),
    )(tiles, begin, features)


def first(counts, x, start):
    vmem = pl.BlockSpec(memory_space=pltpu.VMEM)
    hbm = pl.BlockSpec(memory_space=pltpu.HBM)
    dma = pltpu.SemaphoreType.DMA
    return pl.pallas_call(
        features_kernel,
        out_shape=(
            jax.ShapeDtypeStruct((BP, ROWS * COLS), BF16),
            jax.ShapeDtypeStruct((128, 8, 128), F32),
            jax.ShapeDtypeStruct((RANK, 512), F32),
        ),
        in_specs=[pl.BlockSpec(memory_space=pltpu.SMEM), hbm, hbm],
        out_specs=(hbm, vmem, vmem),
        scratch_shapes=[
            pltpu.VMEM((ROWS * (BP + 2), COLS), BF16),
            pltpu.VMEM((HR, COLS), BF16),
            pltpu.VMEM((HR, COLS), BF16),
            pltpu.VMEM((HR, COLS), BF16),
            pltpu.VMEM((HR, COLS), BF16),
            pltpu.VMEM((BP, ROWS * COLS), BF16),
            pltpu.VMEM((192 * CHUNK, COLS), BF16),
            pltpu.VMEM((192 * CHUNK, COLS), BF16),
            pltpu.VMEM((768, 256), BF16),
            pltpu.VMEM((512, 128), BF16),
            pltpu.VMEM((4, BP, COLS), F32),
            pltpu.VMEM((BP, 512), F32),
            pltpu.VMEM((128, 8, 128), F32),
            pltpu.VMEM((64, 8, 128), F32),
            pltpu.VMEM((63, 8, 128), F32),
            pltpu.VMEM((128, 8, 128), F32),
            pltpu.VMEM((RANK, BANDS), F32),
            dma((CHUNKS,)),
            dma,
            dma((CHUNKS + 1,)),
            dma((CHUNKS + 1,)),
            dma((CHUNKS + 1,)),
            dma((CHUNKS + 1,)),
            dma((4,)),
            dma((4,)),
            pltpu.SemaphoreType.REGULAR((2,)),
            dma,
        ],
        compiler_params=pltpu.CompilerParams(
            collective_id=0, has_side_effects=True, vmem_limit_bytes=53 * 2**20
        ),
    )(counts, x, start.T)


def on_device(radiance, counts, start):
    x = radiance.reshape(BANDS * ROWS, COLS)
    features, tiles, begin = first(counts, x, start)
    projector, scores = second(tiles, begin, features)
    return projector, scores.reshape(1, RANK, ROWS, COLS)


def solution(mesh):
    return jax.shard_map(
        on_device,
        mesh=mesh,
        in_specs=(P("line", None, "track", None), P("line", "track"), P()),
        out_specs=(P(), P("line", None, "track", None)),
        check_vma=False,
    )
```

```python
import functools

import jax
import jax.numpy as jnp
from jax import lax
from jax.experimental import pallas as pl
from jax.experimental.pallas import tpu as pltpu
from jax.sharding import PartitionSpec as P

MESH = pl.DeviceIdType.MESH
F32 = jnp.float32
BF16 = jnp.bfloat16

BANDS = 425
BP = 432
GROUPS = BP // 16
RANK = 64
ITERS = 6
ROWS = 16
COLS = 384
TILES = 16
CHUNK = 3
CHUNKS = GROUPS // CHUNK
SENT = [CHUNK] * (CHUNKS - 1) + [CHUNK - 1, 1]
HR = 16 + 2 * BP + 16
EDGE = (0, 1, 14, 15)
BIN = lambda dist: jnp.where(dist == 0, 6.0, jnp.where(dist == 1, 4.0, jnp.where(dist == 2, 1.0, 0.0)))
NT = (((1,), (1,)), ((), ()))
LOWER = [(rt, ct) for ct in range(4) for rt in range(16 * ct, BP // 8)]


def iotas(shape):
    return lax.broadcasted_iota(jnp.int32, shape, 0), lax.broadcasted_iota(jnp.int32, shape, 1)


def banded(rows, cols, shift):
    ri, ci = iotas((rows, cols))
    return BIN(jnp.abs(ri + shift - ci)).astype(BF16)


def split2(t, hi_ref, lo_ref, rows):
    hi = t.astype(BF16)
    hi_ref[rows, :] = hi
    lo_ref[rows, :] = (t - hi.astype(F32)).astype(BF16)


def smooth_cols(hi_ref, lo_ref, wl_ref, wr_ref, rows):
    hi, lo = hi_ref[0:rows, :], lo_ref[0:rows, :]
    left = jnp.concatenate([hi[:, 0:256], lo[:, 0:256], hi[:, 256:384], lo[:, 256:384]], axis=1)
    right = jnp.concatenate([hi[:, 128:384], lo[:, 128:384]], axis=1)
    return (
        jnp.dot(left, wl_ref[...], preferred_element_type=F32),
        jnp.dot(right, wr_ref[...], preferred_element_type=F32),
    )


def split3(a):
    hi = a.astype(BF16)
    rest = a - hi.astype(F32)
    mid = rest.astype(BF16)
    low = (rest - mid.astype(F32)).astype(BF16)
    return hi, mid, low


def dot6(a, b, dims):
    n = a.shape[0]
    parts = jnp.concatenate(split3(a), axis=0)
    one = lax.dot_general(parts, b[0], dims, preferred_element_type=F32)
    two = lax.dot_general(parts[: 2 * n], b[1], dims, preferred_element_type=F32)
    three = lax.dot_general(parts[:n], b[2], dims, preferred_element_type=F32)
    return one[:n] + (((one[2 * n :] + two[n:]) + three) + (one[n : 2 * n] + two[:n]))


NN = (((1,), (0,)), ((), ()))


def inverse_factor(s):
    ri, ci = iotas((8, 128))
    spread = lambda v, k: jnp.broadcast_to(v[k : k + 1], (8, 128))
    rows = [s[8 * i : 8 * i + 8] + (ci == ri + 64 + 8 * i).astype(F32) for i in range(8)]

    def columns(p, i):
        return [
            jnp.take_along_axis(rows[i], jnp.full((8, 128), 8 * p + l, jnp.int32), axis=1, mode="promise_in_bounds")
            for l in range(8)
        ]

    ahead = columns(0, 0)
    for p in range(8):
        pivots = jnp.ones((8, 128), F32)
        cols, steps = ahead + (columns(p + 1, p) if p < 7 else []), []
        width = len(cols)
        for k in range(8):
            pivot = spread(cols[k], k)
            pivots = jnp.where(ri == k, pivot, pivots)
            inv = 1.0 / pivot
            heads = [spread(cols[l], k) for l in range(k + 1, width)]
            row = spread(rows[p], k)
            steps.append((heads, row, inv))
            if k < 7:
                under = jnp.where(ri > k, cols[k], 0.0)
                m = under * inv
                cols[k + 1] = cols[k + 1] - (under * heads[0]) * inv
                for l in range(k + 2, width):
                    cols[l] = cols[l] - m * heads[l - k - 1]
                rows[p] = rows[p] - m * row
        for i in range(p + 1, 8):
            cols = columns(p, i) + (columns(p + 1, i) if i == p + 1 else [])
            for k, (heads, row, inv) in enumerate(steps):
                m = cols[k] * inv
                for l in range(k + 1, len(cols)):
                    cols[l] = cols[l] - m * heads[l - k - 1]
                rows[i] = rows[i] - m * row
            if i == p + 1:
                ahead = cols[8:]
        rows[p] = rows[p] * lax.rsqrt(pivots)
    return jnp.concatenate(rows, axis=0)


def inner(t):
    zeros = jnp.zeros((RANK, 512), BF16)
    return dot6(t, tuple(jnp.concatenate([p, zeros], axis=0) for p in split3(t)), NT)


def apply(w, t):
    zeros = jnp.zeros((RANK, 512), BF16)
    return dot6(w, tuple(jnp.concatenate([zeros, p], axis=0) for p in split3(t)), NN)


def features_kernel(
    counts_ref, x_hbm, start_hbm, f_hbm, g_ref, b_ref,
    xs, su, sd, hu, hd, fs, th, tl, wl, wr, tb, gs, pk, r1, r2, ag, st,
    x_sem, f_sem, su_sem, sd_sem, hu_sem, hd_sem, ex_send, ex_recv, line_sem, st_sem,
):
    line, track = lax.axis_index("line"), lax.axis_index("track")
    y, core = line // 2, line % 2
    xx, z = track // 4, track % 4
    sibling = (2 * y + 1 - core, track)

    here = (xx, y, z)
    near = [[lax.rem(base + step, 4) for step in range(4)] for base in here]

    def peer(*steps):
        px, py, pz = (near[i][steps[i]] for i in range(3))
        return 16 * px + 4 * py + pz, (2 * py + core, 4 * px + pz)

    on_axis = [[peer(*[step if i == axis else 0 for i in range(3)])[1] for step in (1, 2, 3)] for axis in range(3)]
    others = [(i, j, k) for i in range(4) for j in range(4) for k in range(4)][1:]
    others.sort(key=lambda steps: -sum(min(v, 4 - v) for v in steps))

    before, after = (line, lax.rem(track + TILES - 1, TILES)), (line, lax.rem(track + 1, TILES))
    greeted = [sibling, before, after] + on_axis[0] + on_axis[1] + on_axis[2]

    crow = 256 * CHUNK

    def load(j):
        n = crow if j < CHUNKS - 1 else ROWS * BANDS - crow * (CHUNKS - 1)
        return pltpu.make_async_copy(
            x_hbm.at[pl.ds(crow * j, n)], xs.at[pl.ds(16 + crow * j, n)], x_sem.at[j]
        )

    for j in range(CHUNKS):
        load(j).start()
    st_copy = pltpu.make_async_copy(start_hbm, st, st_sem)
    st_copy.start()

    barrier = pltpu.get_barrier_semaphore()
    for device in greeted:
        pl.semaphore_signal(barrier, inc=1, device_id=device, device_id_type=MESH)

    xs[0:16, :] = jnp.zeros((16, COLS), BF16)
    tail = ROWS * (BANDS + 1)
    xs[tail : ROWS * (BP + 2), :] = jnp.zeros((ROWS * (BP + 2) - tail, COLS), BF16)
    for h in (hu, hd):
        h[0:16, :] = jnp.zeros((16, COLS), BF16)
        h[HR - 16 : HR, :] = jnp.zeros((16, COLS), BF16)

    cnt = counts_ref[0, 0]
    ri, ci = iotas((64, 256))
    want = jnp.where(ri < 32, ri & 1, 14 + (ri & 1))
    sel = ((((ri & 31) >> 1) == (ci >> 4)) & (want == (ci & 15)) & (want < cnt)).astype(F32).astype(BF16)

    def halo(j):
        if isinstance(j, int):
            rows = pl.ds(16 + 32 * sum(SENT[:j]), 32 * SENT[j])
        else:
            rows = pl.ds(pl.multiple_of(16 + 32 * CHUNK * j, 16), 32 * CHUNK)
        first = pltpu.make_async_remote_copy(
            src_ref=su.at[rows], dst_ref=hd.at[rows], send_sem=su_sem.at[j], recv_sem=hd_sem.at[j],
            device_id=before, device_id_type=MESH,
        )
        last = pltpu.make_async_remote_copy(
            src_ref=sd.at[rows], dst_ref=hu.at[rows], send_sem=sd_sem.at[j], recv_sem=hu_sem.at[j],
            device_id=after, device_id_type=MESH,
        )
        return first, last

    for j in range(len(SENT)):
        if j < CHUNKS:
            load(j).wait()
        for g in range(sum(SENT[:j]), sum(SENT[: j + 1])):
            picked = jnp.dot(sel, xs[16 + 256 * g : 272 + 256 * g, :], preferred_element_type=F32).astype(BF16)
            su[16 + 32 * g : 48 + 32 * g, :] = picked[0:32]
            sd[16 + 32 * g : 48 + 32 * g, :] = picked[32:64]
        if j == 0:
            pl.semaphore_wait(barrier, len(greeted))
            for device in on_axis[1]:
                pl.semaphore_signal(line_sem.at[0], inc=1, device_id=device, device_id_type=MESH)
        for copy in halo(j):
            copy.start()

    ri, ci = iotas((128, 160))
    r, b, bi, rr = ri >> 3, ri & 7, ci >> 4, ci & 15
    sign = (bi == b + 2).astype(F32) - (bi == b).astype(F32)
    wt = jnp.where((r < cnt) & (rr < cnt), BIN(jnp.abs(rr - r)), 0.0)
    body = (sign * wt * (1.0 / 512.0)).astype(BF16)

    ri, ci = iotas((64, 128))
    q, b = ri >> 4, ri & 15
    r = jnp.where(q < 2, q, q + 12)
    up = ci < 64
    cj = ci & 63
    bi, rr = cj >> 1, jnp.where(up, (cj & 1) - 2, (cj & 1) + 16)
    sign = (bi == b + 9).astype(F32) - (bi == b + 7).astype(F32)
    have = jnp.where(up, track, TILES - 1 - track) > 0
    wt = jnp.where((r < cnt) & have, BIN(jnp.abs(rr - r)), 0.0)
    rim = (sign * wt * (1.0 / 512.0)).astype(BF16)

    wl[0:256, :] = banded(256, 256, 0)
    wl[256:512, :] = banded(256, 256, 0)
    wl[512:640, :] = banded(128, 256, 256)
    wl[640:768, :] = banded(128, 256, 256)
    wr[0:256, :] = banded(256, 128, -128)
    wr[256:512, :] = banded(256, 128, -128)

    gs[:, 384:512] = jnp.zeros((BP, 128), F32)

    def interior_step(s, carry):
        for u in range(2 * CHUNK):
            at = pl.multiple_of(16 * CHUNK * s + 8 * u, 8)
            xk = xs[pl.ds(pl.multiple_of(256 * CHUNK * s + 128 * u, 128), 160), :]
            t = jnp.dot(body, xk, preferred_element_type=F32)
            for e, row in enumerate(EDGE):
                tb[e, pl.ds(at, 8), :] = t[8 * row : 8 * row + 8]
            split2(t[16:112], th, tl, slice(96 * u, 96 * u + 96))
        wide = smooth_cols(th, tl, wl, wr, 192 * CHUNK)
        for u in range(CHUNK):
            at = pl.ds(pl.multiple_of(16 * CHUNK * s + 16 * u, 16), 16)
            for row in range(2, 14):
                k = 192 * u + 8 * (row - 2)
                for part, col in zip(wide, (row * COLS, row * COLS + 256)):
                    both = jnp.concatenate([part[k : k + 8], part[k + 96 : k + 104]], axis=0)
                    fs[at, col : col + part.shape[1]] = both.astype(BF16)
        return carry

    lax.fori_loop(0, CHUNKS, interior_step, 0)

    pl.semaphore_wait(line_sem.at[0], 3)
    for device in on_axis[2]:
        pl.semaphore_signal(line_sem.at[1], inc=1, device_id=device, device_id_type=MESH)

    def outer(lo, hi):
        a = fs[:, lo:hi]
        left = lax.dot_general(a, a[0:256], NT, preferred_element_type=F32)
        right = lax.dot_general(a[256:BP], a[256:BP], NT, preferred_element_type=F32)
        return left, right

    left, right = outer(2 * COLS, 6 * COLS)
    gs[:, 0:256] = left
    gs[256:BP, 256:BP] = right
    for k in (6, 10):
        left, right = outer(k * COLS, (k + 4) * COLS)
        gs[:, 0:256] += left
        gs[256:BP, 256:BP] += right

    def edges(first, count):
        for u in range(count):
            at = pl.multiple_of(16 * (first + u), 16)
            src = pl.ds(pl.multiple_of(32 * (first + u), 32), 64)
            halos = jnp.concatenate([hu[src, :], hd[src, :]], axis=0)
            t = jnp.dot(rim, halos, preferred_element_type=F32) + tb[:, pl.ds(at, 16), :].reshape(64, COLS)
            split2(t, th, tl, slice(64 * u, 64 * u + 64))
        wide = smooth_cols(th, tl, wl, wr, 64 * count)
        for u in range(count):
            at = pl.ds(pl.multiple_of(16 * (first + u), 16), 16)
            for e, row in enumerate(EDGE):
                k = 64 * u + 16 * e
                for part, col in zip(wide, (row * COLS, row * COLS + 256)):
                    fs[at, col : col + part.shape[1]] = part[k : k + 16].astype(BF16)

    def edge_step(j, carry):
        for copy in halo(j):
            copy.wait_recv()
        edges(CHUNK * j - 1, CHUNK)
        return carry

    for copy in halo(0):
        copy.wait_recv()
    edges(0, CHUNK - 1)
    lax.fori_loop(1, CHUNKS - 1, edge_step, 0)
    for copy in halo(CHUNKS - 1):
        copy.wait_recv()
    edges(GROUPS - CHUNK - 1, 2)
    for copy in halo(CHUNKS):
        copy.wait_recv()
    edges(GROUPS - 2, 2)

    f_copy = pltpu.make_async_copy(fs, f_hbm, f_sem)
    f_copy.start()

    for k in (0, 14):
        left, right = outer(k * COLS, (k + 2) * COLS)
        gs[:, 0:256] += left
        gs[256:BP, 256:BP] += right

    for t, (rt, ct) in enumerate(LOWER):
        pk[t] = gs[8 * rt : 8 * rt + 8, 128 * ct : 128 * ct + 128]
    for t in range(len(LOWER), 128):
        pk[t] = jnp.zeros((8, 128), F32)

    def send(phase, src, dst, device):
        pltpu.make_async_remote_copy(
            src_ref=src, dst_ref=dst, send_sem=ex_send.at[phase], recv_sem=ex_recv.at[phase],
            device_id=device, device_id_type=MESH,
        ).start()

    def arrived(phase, ref):
        pltpu.make_async_copy(ref, ref, ex_recv.at[phase]).wait()

    half = pl.ds(64 * core, 64)
    mine = 64 * core + 16 * xx + 4 * y + z
    send(0, pk.at[pl.ds(64 * (1 - core), 64)], r1, sibling)
    pl.semaphore_wait(line_sem.at[1], 3)
    arrived(0, r1)
    pk[half] += r1[...]
    for n, steps in enumerate(others):
        chip, device = peer(*steps)
        send(1, pk.at[64 * core + chip], r2.at[n], device)
    st_copy.wait()
    begin = jnp.concatenate([st[...], jnp.zeros((RANK, 512 - BANDS), F32)], axis=1)
    b_ref[...] = apply(inverse_factor(inner(begin)), begin)
    arrived(1, r2)
    ag[mine] = pk[mine] + jnp.sum(r2[...], axis=0)
    for steps in others:
        send(2, ag.at[mine], ag.at[mine], peer(*steps)[1])
    arrived(2, r2)
    send(3, ag.at[half], ag.at[half], sibling)
    arrived(3, r1)
    g_ref[...] = ag[...]

    for phase, ref in enumerate((r1, r2, r2, r1)):
        pltpu.make_async_copy(ref, ref, ex_send.at[phase]).wait()

    def sent(j, carry):
        for copy in halo(j):
            copy.wait_send()
        return carry

    lax.fori_loop(0, CHUNKS - 1, sent, 0)
    for j in (CHUNKS - 1, CHUNKS):
        sent(j, 0)
    f_copy.wait()


def iterate_kernel(g_ref, first_ref, f_hbm, proj_hbm, scores_hbm, gf, gh, gm, gl, tt, fs, sc, pj, f_sem, o_sem, p_sem):
    f_copy = pltpu.make_async_copy(f_hbm, fs, f_sem)
    f_copy.start()

    gf[BP:512, :] = jnp.zeros((512 - BP, 512), F32)
    for t, (rt, ct) in enumerate(LOWER):
        tile = g_ref[t]
        if rt == 53 or ct == 3:
            ri, ci = iotas((8, 128))
            tile = jnp.where((ri + 8 * rt < BANDS) & (ci + 128 * ct < BANDS), tile, 0.0)
        gf[8 * rt : 8 * rt + 8, 128 * ct : 128 * ct + 128] = tile
    for i in range(4):
        for j in range(i):
            gf[128 * j : 128 * j + 128, 128 * i : 128 * i + 128] = gf[
                128 * i : 128 * i + 128, 128 * j : 128 * j + 128
            ].T
    for ref, part in zip((gh, gm, gl), split3(gf[...])):
        ref[...] = part

    tt[...] = dot6(first_ref[...], (gh[...], gm[...], gl[...]), NN)

    def step(i, carry):
        t = tt[...]
        s = inner(t)
        z = dot6(t, (gh[...], gm[...], gl[...]), NN)
        tt[...] = apply(inverse_factor(s), z)
        return carry

    lax.fori_loop(1, ITERS, step, 0)
    t = tt[...]
    basis = apply(inverse_factor(inner(t)), t)

    h, m, l = split3(basis)
    lhs = jnp.concatenate([h, h, m, m], axis=0).astype(F32).T.astype(BF16)
    rhs = jnp.concatenate([h, m, h, m], axis=0)
    proj = jnp.dot(lhs, rhs, preferred_element_type=F32)
    pj[...] = proj[0:BANDS, 0:BANDS]
    p_copy = pltpu.make_async_copy(pj, proj_hbm, p_sem)
    p_copy.start()

    f_copy.wait()
    narrow = h[:, 0:BP]

    out = [
        pltpu.make_async_copy(
            sc.at[pl.ds(RANK * ROWS * i, RANK * ROWS)], scores_hbm.at[:, pl.ds(128 * i, 128)], o_sem.at[i]
        )
        for i in range(3)
    ]
    for i in range(3):
        for r in range(ROWS):
            col = r * COLS + 128 * i
            part = jnp.dot(narrow, fs[:, col : col + 128], preferred_element_type=F32)
            sc[pl.ds(RANK * ROWS * i + r, RANK, stride=ROWS), :] = part
        out[i].start()
    for copy in out:
        copy.wait()
    p_copy.wait()


def second(tiles, begin, features):
    vmem = pl.BlockSpec(memory_space=pltpu.VMEM)
    hbm = pl.BlockSpec(memory_space=pltpu.HBM)
    dma = pltpu.SemaphoreType.DMA
    return pl.pallas_call(
        iterate_kernel,
        out_shape=(
            jax.ShapeDtypeStruct((BANDS, BANDS), F32),
            jax.ShapeDtypeStruct((RANK * ROWS, COLS), F32),
        ),
        in_specs=[vmem, vmem, hbm],
        out_specs=(hbm, hbm),
        scratch_shapes=[
            pltpu.VMEM((512, 512), F32),
            pltpu.VMEM((512, 512), BF16),
            pltpu.VMEM((512, 512), BF16),
            pltpu.VMEM((512, 512), BF16),
            pltpu.VMEM((RANK, 512), F32),
            pltpu.VMEM((BP, ROWS * COLS), BF16),
            pltpu.VMEM((3 * RANK * ROWS, 128), F32),
            pltpu.VMEM((BANDS, BANDS), F32),
            dma,
            dma((3,)),
            dma,
        ],
        compiler_params=pltpu.CompilerParams(vmem_limit_bytes=53 * 2**20),
    )(tiles, begin, features)


def first(counts, x, start):
    vmem = pl.BlockSpec(memory_space=pltpu.VMEM)
    hbm = pl.BlockSpec(memory_space=pltpu.HBM)
    dma = pltpu.SemaphoreType.DMA
    return pl.pallas_call(
        features_kernel,
        out_shape=(
            jax.ShapeDtypeStruct((BP, ROWS * COLS), BF16),
            jax.ShapeDtypeStruct((128, 8, 128), F32),
            jax.ShapeDtypeStruct((RANK, 512), F32),
        ),
        in_specs=[pl.BlockSpec(memory_space=pltpu.SMEM), hbm, hbm],
        out_specs=(hbm, vmem, vmem),
        scratch_shapes=[
            pltpu.VMEM((ROWS * (BP + 2), COLS), BF16),
            pltpu.VMEM((HR, COLS), BF16),
            pltpu.VMEM((HR, COLS), BF16),
            pltpu.VMEM((HR, COLS), BF16),
            pltpu.VMEM((HR, COLS), BF16),
            pltpu.VMEM((BP, ROWS * COLS), BF16),
            pltpu.VMEM((192 * CHUNK, COLS), BF16),
            pltpu.VMEM((192 * CHUNK, COLS), BF16),
            pltpu.VMEM((768, 256), BF16),
            pltpu.VMEM((512, 128), BF16),
            pltpu.VMEM((4, BP, COLS), F32),
            pltpu.VMEM((BP, 512), F32),
            pltpu.VMEM((128, 8, 128), F32),
            pltpu.VMEM((64, 8, 128), F32),
            pltpu.VMEM((63, 8, 128), F32),
            pltpu.VMEM((128, 8, 128), F32),
            pltpu.VMEM((RANK, BANDS), F32),
            dma((CHUNKS,)),
            dma,
            dma((CHUNKS + 1,)),
            dma((CHUNKS + 1,)),
            dma((CHUNKS + 1,)),
            dma((CHUNKS + 1,)),
            dma((4,)),
            dma((4,)),
            pltpu.SemaphoreType.REGULAR((2,)),
            dma,
        ],
        compiler_params=pltpu.CompilerParams(
            collective_id=0, has_side_effects=True, vmem_limit_bytes=53 * 2**20
        ),
    )(counts, x, start.T)


def on_device(radiance, counts, start):
    x = radiance.reshape(BANDS * ROWS, COLS)
    features, tiles, begin = first(counts, x, start)
    projector, scores = second(tiles, begin, features)
    return projector, scores.reshape(1, RANK, ROWS, COLS)


def solution(mesh):
    return jax.shard_map(
        on_device,
        mesh=mesh,
        in_specs=(P("line", None, "track", None), P("line", "track"), P()),
        out_specs=(P(), P("line", None, "track", None)),
        check_vma=False,
    )
```

```python
import functools

import jax
import jax.numpy as jnp
from jax import lax
from jax.experimental import pallas as pl
from jax.experimental.pallas import tpu as pltpu
from jax.sharding import PartitionSpec as P

MESH = pl.DeviceIdType.MESH
F32 = jnp.float32
BF16 = jnp.bfloat16

BANDS = 425
BP = 432
GROUPS = BP // 16
RANK = 64
ITERS = 6
ROWS = 16
COLS = 384
TILES = 16
CHUNK = 3
CHUNKS = GROUPS // CHUNK
SENT = [CHUNK] * (CHUNKS - 1) + [CHUNK - 1, 1]
HR = 16 + 2 * BP + 16
EDGE = (0, 1, 14, 15)
BIN = lambda dist: jnp.where(dist == 0, 6.0, jnp.where(dist == 1, 4.0, jnp.where(dist == 2, 1.0, 0.0)))
NT = (((1,), (1,)), ((), ()))
LOWER = [(rt, ct) for ct in range(4) for rt in range(16 * ct, BP // 8)]


def iotas(shape):
    return lax.broadcasted_iota(jnp.int32, shape, 0), lax.broadcasted_iota(jnp.int32, shape, 1)


def banded(rows, cols, shift):
    ri, ci = iotas((rows, cols))
    return BIN(jnp.abs(ri + shift - ci)).astype(BF16)


def split2(t, hi_ref, lo_ref, rows):
    hi = t.astype(BF16)
    hi_ref[rows, :] = hi
    lo_ref[rows, :] = (t - hi.astype(F32)).astype(BF16)


def smooth_cols(hi_ref, lo_ref, wl_ref, wr_ref, rows):
    hi, lo = hi_ref[0:rows, :], lo_ref[0:rows, :]
    left = jnp.concatenate([hi[:, 0:256], lo[:, 0:256], hi[:, 256:384], lo[:, 256:384]], axis=1)
    right = jnp.concatenate([hi[:, 128:384], lo[:, 128:384]], axis=1)
    return (
        jnp.dot(left, wl_ref[...], preferred_element_type=F32),
        jnp.dot(right, wr_ref[...], preferred_element_type=F32),
    )


def split3(a):
    hi = a.astype(BF16)
    rest = a - hi.astype(F32)
    mid = rest.astype(BF16)
    low = (rest - mid.astype(F32)).astype(BF16)
    return hi, mid, low


def dot6(a, b, dims):
    n = a.shape[0]
    parts = jnp.concatenate(split3(a), axis=0)
    one = lax.dot_general(parts, b[0], dims, preferred_element_type=F32)
    two = lax.dot_general(parts[: 2 * n], b[1], dims, preferred_element_type=F32)
    three = lax.dot_general(parts[:n], b[2], dims, preferred_element_type=F32)
    return one[:n] + (((one[2 * n :] + two[n:]) + three) + (one[n : 2 * n] + two[:n]))


NN = (((1,), (0,)), ((), ()))


def inverse_factor(s):
    ri, ci = iotas((8, 128))
    spread = lambda v, k: jnp.broadcast_to(v[k : k + 1], (8, 128))
    rows = [s[8 * i : 8 * i + 8] + (ci == ri + 64 + 8 * i).astype(F32) for i in range(8)]

    def columns(p, i):
        return [
            jnp.take_along_axis(rows[i], jnp.full((8, 128), 8 * p + l, jnp.int32), axis=1, mode="promise_in_bounds")
            for l in range(8)
        ]

    ahead = columns(0, 0)
    for p in range(8):
        pivots = jnp.ones((8, 128), F32)
        cols, steps = ahead + (columns(p + 1, p) if p < 7 else []), []
        width = len(cols)
        for k in range(8):
            pivot = spread(cols[k], k)
            pivots = jnp.where(ri == k, pivot, pivots)
            inv = 1.0 / pivot
            heads = [spread(cols[l], k) for l in range(k + 1, width)]
            row = spread(rows[p], k)
            steps.append((heads, row, inv))
            if k < 7:
                under = jnp.where(ri > k, cols[k], 0.0)
                m = under * inv
                cols[k + 1] = cols[k + 1] - (under * heads[0]) * inv
                for l in range(k + 2, width):
                    cols[l] = cols[l] - m * heads[l - k - 1]
                rows[p] = rows[p] - m * row
        for i in range(p + 1, 8):
            cols = columns(p, i) + (columns(p + 1, i) if i == p + 1 else [])
            for k, (heads, row, inv) in enumerate(steps):
                m = cols[k] * inv
                for l in range(k + 1, len(cols)):
                    cols[l] = cols[l] - m * heads[l - k - 1]
                rows[i] = rows[i] - m * row
            if i == p + 1:
                ahead = cols[8:]
        rows[p] = rows[p] * lax.rsqrt(pivots)
    return jnp.concatenate(rows, axis=0)


def inner(t):
    zeros = jnp.zeros((RANK, 512), BF16)
    return dot6(t, tuple(jnp.concatenate([p, zeros], axis=0) for p in split3(t)), NT)


def apply(w, t):
    zeros = jnp.zeros((RANK, 512), BF16)
    return dot6(w, tuple(jnp.concatenate([zeros, p], axis=0) for p in split3(t)), NN)


def features_kernel(
    counts_ref, x_hbm, start_hbm, f_hbm, g0, g1, g2, g3, b_ref,
    xs, su, sd, hu, hd, fs, th, tl, wl, wr, tb, gs, pk, r1, r2, ag, st,
    x_sem, f_sem, su_sem, sd_sem, hu_sem, hd_sem, ex_send, ex_recv, line_sem, st_sem,
):
    line, track = lax.axis_index("line"), lax.axis_index("track")
    y, core = line // 2, line % 2
    xx, z = track // 4, track % 4
    sibling = (2 * y + 1 - core, track)

    here = (xx, y, z)
    near = [[lax.rem(base + step, 4) for step in range(4)] for base in here]

    def peer(*steps):
        px, py, pz = (near[i][steps[i]] for i in range(3))
        return 16 * px + 4 * py + pz, (2 * py + core, 4 * px + pz)

    on_axis = [[peer(*[step if i == axis else 0 for i in range(3)])[1] for step in (1, 2, 3)] for axis in range(3)]
    others = [(i, j, k) for i in range(4) for j in range(4) for k in range(4)][1:]
    others.sort(key=lambda steps: -sum(min(v, 4 - v) for v in steps))

    before, after = (line, lax.rem(track + TILES - 1, TILES)), (line, lax.rem(track + 1, TILES))
    greeted = [sibling, before, after] + on_axis[0] + on_axis[1] + on_axis[2]

    crow = 256 * CHUNK

    def load(j):
        n = crow if j < CHUNKS - 1 else ROWS * BANDS - crow * (CHUNKS - 1)
        return pltpu.make_async_copy(
            x_hbm.at[pl.ds(crow * j, n)], xs.at[pl.ds(16 + crow * j, n)], x_sem.at[j]
        )

    for j in range(CHUNKS):
        load(j).start()
    st_copy = pltpu.make_async_copy(start_hbm, st, st_sem)
    st_copy.start()

    barrier = pltpu.get_barrier_semaphore()
    for device in greeted:
        pl.semaphore_signal(barrier, inc=1, device_id=device, device_id_type=MESH)

    xs[0:16, :] = jnp.zeros((16, COLS), BF16)
    tail = ROWS * (BANDS + 1)
    xs[tail : ROWS * (BP + 2), :] = jnp.zeros((ROWS * (BP + 2) - tail, COLS), BF16)
    for h in (hu, hd):
        h[0:16, :] = jnp.zeros((16, COLS), BF16)
        h[HR - 16 : HR, :] = jnp.zeros((16, COLS), BF16)

    cnt = counts_ref[0, 0]
    ri, ci = iotas((64, 256))
    want = jnp.where(ri < 32, ri & 1, 14 + (ri & 1))
    sel = ((((ri & 31) >> 1) == (ci >> 4)) & (want == (ci & 15)) & (want < cnt)).astype(F32).astype(BF16)

    def halo(j):
        if isinstance(j, int):
            rows = pl.ds(16 + 32 * sum(SENT[:j]), 32 * SENT[j])
        else:
            rows = pl.ds(pl.multiple_of(16 + 32 * CHUNK * j, 16), 32 * CHUNK)
        first = pltpu.make_async_remote_copy(
            src_ref=su.at[rows], dst_ref=hd.at[rows], send_sem=su_sem.at[j], recv_sem=hd_sem.at[j],
            device_id=before, device_id_type=MESH,
        )
        last = pltpu.make_async_remote_copy(
            src_ref=sd.at[rows], dst_ref=hu.at[rows], send_sem=sd_sem.at[j], recv_sem=hu_sem.at[j],
            device_id=after, device_id_type=MESH,
        )
        return first, last

    for j in range(len(SENT)):
        if j < CHUNKS:
            load(j).wait()
        for g in range(sum(SENT[:j]), sum(SENT[: j + 1])):
            picked = jnp.dot(sel, xs[16 + 256 * g : 272 + 256 * g, :], preferred_element_type=F32).astype(BF16)
            su[16 + 32 * g : 48 + 32 * g, :] = picked[0:32]
            sd[16 + 32 * g : 48 + 32 * g, :] = picked[32:64]
        if j == 0:
            pl.semaphore_wait(barrier, len(greeted))
            for device in on_axis[1]:
                pl.semaphore_signal(line_sem.at[0], inc=1, device_id=device, device_id_type=MESH)
        for copy in halo(j):
            copy.start()

    ri, ci = iotas((128, 160))
    r, b, bi, rr = ri >> 3, ri & 7, ci >> 4, ci & 15
    sign = (bi == b + 2).astype(F32) - (bi == b).astype(F32)
    wt = jnp.where((r < cnt) & (rr < cnt), BIN(jnp.abs(rr - r)), 0.0)
    body = (sign * wt * (1.0 / 512.0)).astype(BF16)

    ri, ci = iotas((64, 128))
    q, b = ri >> 4, ri & 15
    r = jnp.where(q < 2, q, q + 12)
    up = ci < 64
    cj = ci & 63
    bi, rr = cj >> 1, jnp.where(up, (cj & 1) - 2, (cj & 1) + 16)
    sign = (bi == b + 9).astype(F32) - (bi == b + 7).astype(F32)
    have = jnp.where(up, track, TILES - 1 - track) > 0
    wt = jnp.where((r < cnt) & have, BIN(jnp.abs(rr - r)), 0.0)
    rim = (sign * wt * (1.0 / 512.0)).astype(BF16)

    wl[0:256, :] = banded(256, 256, 0)
    wl[256:512, :] = banded(256, 256, 0)
    wl[512:640, :] = banded(128, 256, 256)
    wl[640:768, :] = banded(128, 256, 256)
    wr[0:256, :] = banded(256, 128, -128)
    wr[256:512, :] = banded(256, 128, -128)

    gs[:, 384:512] = jnp.zeros((BP, 128), F32)

    def interior_step(s, carry):
        for u in range(2 * CHUNK):
            at = pl.multiple_of(16 * CHUNK * s + 8 * u, 8)
            xk = xs[pl.ds(pl.multiple_of(256 * CHUNK * s + 128 * u, 128), 160), :]
            t = jnp.dot(body, xk, preferred_element_type=F32)
            for e, row in enumerate(EDGE):
                tb[e, pl.ds(at, 8), :] = t[8 * row : 8 * row + 8]
            split2(t[16:112], th, tl, slice(96 * u, 96 * u + 96))
        wide = smooth_cols(th, tl, wl, wr, 192 * CHUNK)
        for u in range(CHUNK):
            at = pl.ds(pl.multiple_of(16 * CHUNK * s + 16 * u, 16), 16)
            for row in range(2, 14):
                k = 192 * u + 8 * (row - 2)
                for part, col in zip(wide, (row * COLS, row * COLS + 256)):
                    both = jnp.concatenate([part[k : k + 8], part[k + 96 : k + 104]], axis=0)
                    fs[at, col : col + part.shape[1]] = both.astype(BF16)
        return carry

    lax.fori_loop(0, CHUNKS, interior_step, 0)

    pl.semaphore_wait(line_sem.at[0], 3)
    for device in on_axis[2]:
        pl.semaphore_signal(line_sem.at[1], inc=1, device_id=device, device_id_type=MESH)

    def outer(lo, hi):
        a = fs[:, lo:hi]
        left = lax.dot_general(a, a[0:256], NT, preferred_element_type=F32)
        right = lax.dot_general(a[256:BP], a[256:BP], NT, preferred_element_type=F32)
        return left, right

    left, right = outer(2 * COLS, 6 * COLS)
    gs[:, 0:256] = left
    gs[256:BP, 256:BP] = right
    for k in (6, 10):
        left, right = outer(k * COLS, (k + 4) * COLS)
        gs[:, 0:256] += left
        gs[256:BP, 256:BP] += right

    def edges(first, count):
        for u in range(count):
            at = pl.multiple_of(16 * (first + u), 16)
            src = pl.ds(pl.multiple_of(32 * (first + u), 32), 64)
            halos = jnp.concatenate([hu[src, :], hd[src, :]], axis=0)
            t = jnp.dot(rim, halos, preferred_element_type=F32) + tb[:, pl.ds(at, 16), :].reshape(64, COLS)
            split2(t, th, tl, slice(64 * u, 64 * u + 64))
        wide = smooth_cols(th, tl, wl, wr, 64 * count)
        for u in range(count):
            at = pl.ds(pl.multiple_of(16 * (first + u), 16), 16)
            for e, row in enumerate(EDGE):
                k = 64 * u + 16 * e
                for part, col in zip(wide, (row * COLS, row * COLS + 256)):
                    fs[at, col : col + part.shape[1]] = part[k : k + 16].astype(BF16)

    def edge_step(j, carry):
        for copy in halo(j):
            copy.wait_recv()
        edges(CHUNK * j - 1, CHUNK)
        return carry

    for copy in halo(0):
        copy.wait_recv()
    edges(0, CHUNK - 1)
    lax.fori_loop(1, CHUNKS - 1, edge_step, 0)
    for copy in halo(CHUNKS - 1):
        copy.wait_recv()
    edges(GROUPS - CHUNK - 1, 2)
    for copy in halo(CHUNKS):
        copy.wait_recv()
    edges(GROUPS - 2, 2)

    f_copy = pltpu.make_async_copy(fs, f_hbm, f_sem)
    f_copy.start()

    for k in (0, 14):
        left, right = outer(k * COLS, (k + 2) * COLS)
        gs[:, 0:256] += left
        gs[256:BP, 256:BP] += right

    for t, (rt, ct) in enumerate(LOWER):
        pk[t] = gs[8 * rt : 8 * rt + 8, 128 * ct : 128 * ct + 128]
    for t in range(len(LOWER), 128):
        pk[t] = jnp.zeros((8, 128), F32)

    def send(phase, src, dst, device):
        pltpu.make_async_remote_copy(
            src_ref=src, dst_ref=dst, send_sem=ex_send.at[phase], recv_sem=ex_recv.at[phase],
            device_id=device, device_id_type=MESH,
        ).start()

    def arrived(phase, ref):
        pltpu.make_async_copy(ref, ref, ex_recv.at[phase]).wait()

    half = pl.ds(64 * core, 64)
    mine = 64 * core + 16 * xx + 4 * y + z
    send(0, pk.at[pl.ds(64 * (1 - core), 64)], r1, sibling)
    pl.semaphore_wait(line_sem.at[1], 3)
    arrived(0, r1)
    pk[half] += r1[...]
    for n, steps in enumerate(others):
        chip, device = peer(*steps)
        send(1, pk.at[64 * core + chip], r2.at[n], device)
    st_copy.wait()
    begin = jnp.concatenate([st[...], jnp.zeros((RANK, 512 - BANDS), F32)], axis=1)
    b_ref[...] = apply(inverse_factor(inner(begin)), begin)
    arrived(1, r2)
    ag[mine] = pk[mine] + jnp.sum(r2[...], axis=0)
    for steps in others:
        send(2, ag.at[mine], ag.at[mine], peer(*steps)[1])
    arrived(2, r2)
    send(3, ag.at[half], ag.at[half], sibling)
    arrived(3, r1)
    for n, out in enumerate((g0, g1, g2, g3)):
        out[...] = ag[32 * n : 32 * n + 32]

    for phase, ref in enumerate((r1, r2, r2, r1)):
        pltpu.make_async_copy(ref, ref, ex_send.at[phase]).wait()

    def sent(j, carry):
        for copy in halo(j):
            copy.wait_send()
        return carry

    lax.fori_loop(0, CHUNKS - 1, sent, 0)
    for j in (CHUNKS - 1, CHUNKS):
        sent(j, 0)
    f_copy.wait()


def iterate_kernel(g0, g1, g2, g3, first_ref, f_hbm, proj_hbm, scores_hbm, gf, gh, gm, gl, tt, fs, sc, pj, f_sem, o_sem, p_sem):
    f_copy = pltpu.make_async_copy(f_hbm, fs, f_sem)
    f_copy.start()

    gf[BP:512, :] = jnp.zeros((512 - BP, 512), F32)
    for t, (rt, ct) in enumerate(LOWER):
        tile = (g0, g1, g2, g3)[t // 32][t % 32]
        if rt == 53 or ct == 3:
            ri, ci = iotas((8, 128))
            tile = jnp.where((ri + 8 * rt < BANDS) & (ci + 128 * ct < BANDS), tile, 0.0)
        gf[8 * rt : 8 * rt + 8, 128 * ct : 128 * ct + 128] = tile
    for i in range(4):
        for j in range(i):
            gf[128 * j : 128 * j + 128, 128 * i : 128 * i + 128] = gf[
                128 * i : 128 * i + 128, 128 * j : 128 * j + 128
            ].T
    for ref, part in zip((gh, gm, gl), split3(gf[...])):
        ref[...] = part

    tt[...] = dot6(first_ref[...], (gh[...], gm[...], gl[...]), NN)

    def step(i, carry):
        t = tt[...]
        s = inner(t)
        z = dot6(t, (gh[...], gm[...], gl[...]), NN)
        tt[...] = apply(inverse_factor(s), z)
        return carry

    lax.fori_loop(1, ITERS, step, 0)
    t = tt[...]
    basis = apply(inverse_factor(inner(t)), t)

    h, m, l = split3(basis)
    lhs = jnp.concatenate([h, h, m, m], axis=0).astype(F32).T.astype(BF16)
    rhs = jnp.concatenate([h, m, h, m], axis=0)
    proj = jnp.dot(lhs, rhs, preferred_element_type=F32)
    pj[...] = proj[0:BANDS, 0:BANDS]
    p_copy = pltpu.make_async_copy(pj, proj_hbm, p_sem)
    p_copy.start()

    f_copy.wait()
    narrow = h[:, 0:BP]

    out = [
        pltpu.make_async_copy(
            sc.at[pl.ds(RANK * ROWS * i, RANK * ROWS)], scores_hbm.at[:, pl.ds(128 * i, 128)], o_sem.at[i]
        )
        for i in range(3)
    ]
    for i in range(3):
        for r in range(ROWS):
            col = r * COLS + 128 * i
            part = jnp.dot(narrow, fs[:, col : col + 128], preferred_element_type=F32)
            sc[pl.ds(RANK * ROWS * i + r, RANK, stride=ROWS), :] = part
        out[i].start()
    for copy in out:
        copy.wait()
    p_copy.wait()


def second(tiles, begin, features):
    vmem = pl.BlockSpec(memory_space=pltpu.VMEM)
    hbm = pl.BlockSpec(memory_space=pltpu.HBM)
    dma = pltpu.SemaphoreType.DMA
    return pl.pallas_call(
        iterate_kernel,
        out_shape=(
            jax.ShapeDtypeStruct((BANDS, BANDS), F32),
            jax.ShapeDtypeStruct((RANK * ROWS, COLS), F32),
        ),
        in_specs=[*[vmem] * 5, hbm],
        out_specs=(hbm, hbm),
        scratch_shapes=[
            pltpu.VMEM((512, 512), F32),
            pltpu.VMEM((512, 512), BF16),
            pltpu.VMEM((512, 512), BF16),
            pltpu.VMEM((512, 512), BF16),
            pltpu.VMEM((RANK, 512), F32),
            pltpu.VMEM((BP, ROWS * COLS), BF16),
            pltpu.VMEM((3 * RANK * ROWS, 128), F32),
            pltpu.VMEM((BANDS, BANDS), F32),
            dma,
            dma((3,)),
            dma,
        ],
        compiler_params=pltpu.CompilerParams(vmem_limit_bytes=54528 * 1024),
    )(*tiles, begin, features)


def first(counts, x, start):
    vmem = pl.BlockSpec(memory_space=pltpu.VMEM)
    hbm = pl.BlockSpec(memory_space=pltpu.HBM)
    dma = pltpu.SemaphoreType.DMA
    return pl.pallas_call(
        features_kernel,
        out_shape=(
            jax.ShapeDtypeStruct((BP, ROWS * COLS), BF16),
            *[jax.ShapeDtypeStruct((32, 8, 128), F32)] * 4,
            jax.ShapeDtypeStruct((RANK, 512), F32),
        ),
        in_specs=[pl.BlockSpec(memory_space=pltpu.SMEM), hbm, hbm],
        out_specs=(hbm, *[vmem] * 5),
        scratch_shapes=[
            pltpu.VMEM((ROWS * (BP + 2), COLS), BF16),
            pltpu.VMEM((HR, COLS), BF16),
            pltpu.VMEM((HR, COLS), BF16),
            pltpu.VMEM((HR, COLS), BF16),
            pltpu.VMEM((HR, COLS), BF16),
            pltpu.VMEM((BP, ROWS * COLS), BF16),
            pltpu.VMEM((192 * CHUNK, COLS), BF16),
            pltpu.VMEM((192 * CHUNK, COLS), BF16),
            pltpu.VMEM((768, 256), BF16),
            pltpu.VMEM((512, 128), BF16),
            pltpu.VMEM((4, BP, COLS), F32),
            pltpu.VMEM((BP, 512), F32),
            pltpu.VMEM((128, 8, 128), F32),
            pltpu.VMEM((64, 8, 128), F32),
            pltpu.VMEM((63, 8, 128), F32),
            pltpu.VMEM((128, 8, 128), F32),
            pltpu.VMEM((RANK, BANDS), F32),
            dma((CHUNKS,)),
            dma,
            dma((CHUNKS + 1,)),
            dma((CHUNKS + 1,)),
            dma((CHUNKS + 1,)),
            dma((CHUNKS + 1,)),
            dma((4,)),
            dma((4,)),
            pltpu.SemaphoreType.REGULAR((2,)),
            dma,
        ],
        compiler_params=pltpu.CompilerParams(
            collective_id=0, has_side_effects=True, vmem_limit_bytes=54528 * 1024
        ),
    )(counts, x, start.T)


def on_device(radiance, counts, start):
    x = radiance.reshape(BANDS * ROWS, COLS)
    features, *tiles, begin = first(counts, x, start)
    projector, scores = second(tiles, begin, features)
    return projector, scores.reshape(1, RANK, ROWS, COLS)


def solution(mesh):
    return jax.shard_map(
        on_device,
        mesh=mesh,
        in_specs=(P("line", None, "track", None), P("line", "track"), P()),
        out_specs=(P(), P("line", None, "track", None)),
        check_vma=False,
    )
```

```python
import functools

import jax
import jax.numpy as jnp
from jax import lax
from jax.experimental import pallas as pl
from jax.experimental.pallas import tpu as pltpu
from jax.sharding import PartitionSpec as P

MESH = pl.DeviceIdType.MESH
F32 = jnp.float32
BF16 = jnp.bfloat16

BANDS = 425
BP = 432
GROUPS = BP // 16
RANK = 64
ITERS = 6
ROWS = 16
COLS = 384
TILES = 16
CHUNK = 3
CHUNKS = GROUPS // CHUNK
SENT = [CHUNK] * (CHUNKS - 1) + [CHUNK - 1, 1]
HR = 16 + 2 * BP + 16
EDGE = (0, 1, 14, 15)
BIN = lambda dist: jnp.where(dist == 0, 6.0, jnp.where(dist == 1, 4.0, jnp.where(dist == 2, 1.0, 0.0)))
NT = (((1,), (1,)), ((), ()))
LOWER = [(rt, ct) for ct in range(4) for rt in range(16 * ct, BP // 8)]


def iotas(shape):
    return lax.broadcasted_iota(jnp.int32, shape, 0), lax.broadcasted_iota(jnp.int32, shape, 1)


def banded(rows, cols, shift):
    ri, ci = iotas((rows, cols))
    return BIN(jnp.abs(ri + shift - ci)).astype(BF16)


def split2(t, hi_ref, lo_ref, rows):
    hi = t.astype(BF16)
    hi_ref[rows, :] = hi
    lo_ref[rows, :] = (t - hi.astype(F32)).astype(BF16)


def smooth_cols(hi_ref, lo_ref, wl_ref, wr_ref, rows):
    hi, lo = hi_ref[0:rows, :], lo_ref[0:rows, :]
    left = jnp.concatenate([hi[:, 0:256], lo[:, 0:256], hi[:, 256:384], lo[:, 256:384]], axis=1)
    right = jnp.concatenate([hi[:, 128:384], lo[:, 128:384]], axis=1)
    return (
        jnp.dot(left, wl_ref[...], preferred_element_type=F32),
        jnp.dot(right, wr_ref[...], preferred_element_type=F32),
    )


def split3(a):
    hi = a.astype(BF16)
    rest = a - hi.astype(F32)
    mid = rest.astype(BF16)
    low = (rest - mid.astype(F32)).astype(BF16)
    return hi, mid, low


def dot6(a, b, dims):
    n = a.shape[0]
    parts = jnp.concatenate(split3(a), axis=0)
    one = lax.dot_general(parts, b[0], dims, preferred_element_type=F32)
    two = lax.dot_general(parts[: 2 * n], b[1], dims, preferred_element_type=F32)
    three = lax.dot_general(parts[:n], b[2], dims, preferred_element_type=F32)
    return one[:n] + (((one[2 * n :] + two[n:]) + three) + (one[n : 2 * n] + two[:n]))


NN = (((1,), (0,)), ((), ()))


def inverse_factor(s):
    ri, ci = iotas((8, 128))
    spread = lambda v, k: jnp.broadcast_to(v[k : k + 1], (8, 128))
    rows = [s[8 * i : 8 * i + 8] + (ci == ri + 64 + 8 * i).astype(F32) for i in range(8)]

    def columns(p, i):
        return [
            jnp.take_along_axis(rows[i], jnp.full((8, 128), 8 * p + l, jnp.int32), axis=1, mode="promise_in_bounds")
            for l in range(8)
        ]

    ahead = columns(0, 0)
    for p in range(8):
        pivots = jnp.ones((8, 128), F32)
        cols, steps = ahead + (columns(p + 1, p) if p < 7 else []), []
        width = len(cols)
        for k in range(8):
            pivot = spread(cols[k], k)
            pivots = jnp.where(ri == k, pivot, pivots)
            inv = 1.0 / pivot
            heads = [spread(cols[l], k) for l in range(k + 1, width)]
            row = spread(rows[p], k)
            steps.append((heads, row, inv))
            if k < 7:
                under = jnp.where(ri > k, cols[k], 0.0)
                m = under * inv
                cols[k + 1] = cols[k + 1] - (under * heads[0]) * inv
                for l in range(k + 2, width):
                    cols[l] = cols[l] - m * heads[l - k - 1]
                rows[p] = rows[p] - m * row
        for i in range(p + 1, 8):
            cols = columns(p, i) + (columns(p + 1, i) if i == p + 1 else [])
            for k, (heads, row, inv) in enumerate(steps):
                m = cols[k] * inv
                for l in range(k + 1, len(cols)):
                    cols[l] = cols[l] - m * heads[l - k - 1]
                rows[i] = rows[i] - m * row
            if i == p + 1:
                ahead = cols[8:]
        rows[p] = rows[p] * lax.rsqrt(pivots)
    return jnp.concatenate(rows, axis=0)


def inner(t):
    zeros = jnp.zeros((RANK, 512), BF16)
    return dot6(t, tuple(jnp.concatenate([p, zeros], axis=0) for p in split3(t)), NT)


def apply(w, t):
    zeros = jnp.zeros((RANK, 512), BF16)
    return dot6(w, tuple(jnp.concatenate([zeros, p], axis=0) for p in split3(t)), NN)


def features_kernel(
    counts_ref, x_hbm, start_hbm, f_hbm, g0, g1, g2, g3, b_ref,
    xs, su, sd, hu, hd, fs, th, tl, wl, wr, tb, gs, pk, r1, r2, ag, st,
    x_sem, f_sem, su_sem, sd_sem, hu_sem, hd_sem, ex_send, ex_recv, line_sem, st_sem,
):
    line, track = lax.axis_index("line"), lax.axis_index("track")
    y, core = line // 2, line % 2
    xx, z = track // 4, track % 4
    sibling = (2 * y + 1 - core, track)

    here = (xx, y, z)
    near = [[lax.rem(base + step, 4) for step in range(4)] for base in here]

    def peer(*steps):
        px, py, pz = (near[i][steps[i]] for i in range(3))
        return 16 * px + 4 * py + pz, (2 * py + core, 4 * px + pz)

    on_axis = [[peer(*[step if i == axis else 0 for i in range(3)])[1] for step in (1, 2, 3)] for axis in range(3)]
    others = [(i, j, k) for i in range(4) for j in range(4) for k in range(4)][1:]
    others.sort(key=lambda steps: -sum(min(v, 4 - v) for v in steps))

    before, after = (line, lax.rem(track + TILES - 1, TILES)), (line, lax.rem(track + 1, TILES))
    greeted = [sibling, before, after] + on_axis[0] + on_axis[1] + on_axis[2]

    crow = 256 * CHUNK

    def load(j):
        n = crow if j < CHUNKS - 1 else ROWS * BANDS - crow * (CHUNKS - 1)
        return pltpu.make_async_copy(
            x_hbm.at[pl.ds(crow * j, n)], xs.at[pl.ds(16 + crow * j, n)], x_sem.at[j]
        )

    for j in range(CHUNKS):
        load(j).start()
    st_copy = pltpu.make_async_copy(start_hbm, st, st_sem)
    st_copy.start()

    barrier = pltpu.get_barrier_semaphore()
    for device in greeted:
        pl.semaphore_signal(barrier, inc=1, device_id=device, device_id_type=MESH)

    xs[0:16, :] = jnp.zeros((16, COLS), BF16)
    tail = ROWS * (BANDS + 1)
    xs[tail : ROWS * (BP + 2), :] = jnp.zeros((ROWS * (BP + 2) - tail, COLS), BF16)
    for h in (hu, hd):
        h[0:16, :] = jnp.zeros((16, COLS), BF16)
        h[HR - 16 : HR, :] = jnp.zeros((16, COLS), BF16)

    cnt = counts_ref[0, 0]
    ri, ci = iotas((64, 256))
    want = jnp.where(ri < 32, ri & 1, 14 + (ri & 1))
    sel = ((((ri & 31) >> 1) == (ci >> 4)) & (want == (ci & 15)) & (want < cnt)).astype(F32).astype(BF16)

    def halo(j):
        if isinstance(j, int):
            rows = pl.ds(16 + 32 * sum(SENT[:j]), 32 * SENT[j])
        else:
            rows = pl.ds(pl.multiple_of(16 + 32 * CHUNK * j, 16), 32 * CHUNK)
        first = pltpu.make_async_remote_copy(
            src_ref=su.at[rows], dst_ref=hd.at[rows], send_sem=su_sem.at[j], recv_sem=hd_sem.at[j],
            device_id=before, device_id_type=MESH,
        )
        last = pltpu.make_async_remote_copy(
            src_ref=sd.at[rows], dst_ref=hu.at[rows], send_sem=sd_sem.at[j], recv_sem=hu_sem.at[j],
            device_id=after, device_id_type=MESH,
        )
        return first, last

    for j in range(len(SENT)):
        if j < CHUNKS:
            load(j).wait()
        for g in range(sum(SENT[:j]), sum(SENT[: j + 1])):
            picked = jnp.dot(sel, xs[16 + 256 * g : 272 + 256 * g, :], preferred_element_type=F32).astype(BF16)
            su[16 + 32 * g : 48 + 32 * g, :] = picked[0:32]
            sd[16 + 32 * g : 48 + 32 * g, :] = picked[32:64]
        if j == 0:
            pl.semaphore_wait(barrier, len(greeted))
            for device in on_axis[1]:
                pl.semaphore_signal(line_sem.at[0], inc=1, device_id=device, device_id_type=MESH)
        for copy in halo(j):
            copy.start()

    ri, ci = iotas((128, 160))
    r, b, bi, rr = ri >> 3, ri & 7, ci >> 4, ci & 15
    sign = (bi == b + 2).astype(F32) - (bi == b).astype(F32)
    wt = jnp.where((r < cnt) & (rr < cnt), BIN(jnp.abs(rr - r)), 0.0)
    body = (sign * wt * (1.0 / 512.0)).astype(BF16)

    ri, ci = iotas((64, 128))
    q, b = ri >> 4, ri & 15
    r = jnp.where(q < 2, q, q + 12)
    up = ci < 64
    cj = ci & 63
    bi, rr = cj >> 1, jnp.where(up, (cj & 1) - 2, (cj & 1) + 16)
    sign = (bi == b + 9).astype(F32) - (bi == b + 7).astype(F32)
    have = jnp.where(up, track, TILES - 1 - track) > 0
    wt = jnp.where((r < cnt) & have, BIN(jnp.abs(rr - r)), 0.0)
    rim = (sign * wt * (1.0 / 512.0)).astype(BF16)

    wl[0:256, :] = banded(256, 256, 0)
    wl[256:512, :] = banded(256, 256, 0)
    wl[512:640, :] = banded(128, 256, 256)
    wl[640:768, :] = banded(128, 256, 256)
    wr[0:256, :] = banded(256, 128, -128)
    wr[256:512, :] = banded(256, 128, -128)

    gs[:, 384:512] = jnp.zeros((BP, 128), F32)

    def interior_step(s, carry):
        for u in range(2 * CHUNK):
            at = pl.multiple_of(16 * CHUNK * s + 8 * u, 8)
            xk = xs[pl.ds(pl.multiple_of(256 * CHUNK * s + 128 * u, 128), 160), :]
            t = jnp.dot(body, xk, preferred_element_type=F32)
            for e, row in enumerate(EDGE):
                tb[e, pl.ds(at, 8), :] = t[8 * row : 8 * row + 8]
            split2(t[16:112], th, tl, slice(96 * u, 96 * u + 96))
        wide = smooth_cols(th, tl, wl, wr, 192 * CHUNK)
        for u in range(CHUNK):
            at = pl.ds(pl.multiple_of(16 * CHUNK * s + 16 * u, 16), 16)
            for row in range(2, 14):
                k = 192 * u + 8 * (row - 2)
                for part, col in zip(wide, (row * COLS, row * COLS + 256)):
                    both = jnp.concatenate([part[k : k + 8], part[k + 96 : k + 104]], axis=0)
                    fs[at, col : col + part.shape[1]] = both.astype(BF16)
        return carry

    lax.fori_loop(0, CHUNKS, interior_step, 0)

    pl.semaphore_wait(line_sem.at[0], 3)
    for device in on_axis[2]:
        pl.semaphore_signal(line_sem.at[1], inc=1, device_id=device, device_id_type=MESH)

    def outer(a):
        left = lax.dot_general(a, a[0:256], NT, preferred_element_type=F32)
        right = lax.dot_general(a[256:BP], a[256:BP], NT, preferred_element_type=F32)
        return left, right

    left, right = outer(fs[:, 2 * COLS : 6 * COLS])
    gs[:, 0:256] = left
    gs[256:BP, 256:BP] = right
    for k in (6, 10):
        left, right = outer(fs[:, k * COLS : (k + 4) * COLS])
        gs[:, 0:256] += left
        gs[256:BP, 256:BP] += right

    def edges(first, count):
        for u in range(count):
            at = pl.multiple_of(16 * (first + u), 16)
            src = pl.ds(pl.multiple_of(32 * (first + u), 32), 64)
            halos = jnp.concatenate([hu[src, :], hd[src, :]], axis=0)
            t = jnp.dot(rim, halos, preferred_element_type=F32) + tb[:, pl.ds(at, 16), :].reshape(64, COLS)
            split2(t, th, tl, slice(64 * u, 64 * u + 64))
        wide = smooth_cols(th, tl, wl, wr, 64 * count)
        for u in range(count):
            at = pl.ds(pl.multiple_of(16 * (first + u), 16), 16)
            for e, row in enumerate(EDGE):
                k = 64 * u + 16 * e
                for part, col in zip(wide, (row * COLS, row * COLS + 256)):
                    fs[at, col : col + part.shape[1]] = part[k : k + 16].astype(BF16)

    def edge_step(j, carry):
        for copy in halo(j):
            copy.wait_recv()
        edges(CHUNK * j - 1, CHUNK)
        return carry

    for copy in halo(0):
        copy.wait_recv()
    edges(0, CHUNK - 1)
    lax.fori_loop(1, CHUNKS - 1, edge_step, 0)
    for copy in halo(CHUNKS - 1):
        copy.wait_recv()
    edges(GROUPS - CHUNK - 1, 2)
    for copy in halo(CHUNKS):
        copy.wait_recv()
    edges(GROUPS - 2, 2)

    f_copy = pltpu.make_async_copy(fs, f_hbm, f_sem)
    f_copy.start()

    left, right = outer(jnp.concatenate([fs[:, 0 : 2 * COLS], fs[:, 14 * COLS : 16 * COLS]], axis=1))
    gs[:, 0:256] += left
    gs[256:BP, 256:BP] += right

    for t, (rt, ct) in enumerate(LOWER):
        pk[t] = gs[8 * rt : 8 * rt + 8, 128 * ct : 128 * ct + 128]
    for t in range(len(LOWER), 128):
        pk[t] = jnp.zeros((8, 128), F32)

    def send(phase, src, dst, device):
        pltpu.make_async_remote_copy(
            src_ref=src, dst_ref=dst, send_sem=ex_send.at[phase], recv_sem=ex_recv.at[phase],
            device_id=device, device_id_type=MESH,
        ).start()

    def arrived(phase, ref):
        pltpu.make_async_copy(ref, ref, ex_recv.at[phase]).wait()

    half = pl.ds(64 * core, 64)
    mine = 64 * core + 16 * xx + 4 * y + z
    send(0, pk.at[pl.ds(64 * (1 - core), 64)], r1, sibling)
    pl.semaphore_wait(line_sem.at[1], 3)
    arrived(0, r1)
    pk[half] += r1[...]
    for n, steps in enumerate(others):
        chip, device = peer(*steps)
        send(1, pk.at[64 * core + chip], r2.at[n], device)
    st_copy.wait()
    begin = jnp.concatenate([st[...], jnp.zeros((RANK, 512 - BANDS), F32)], axis=1)
    b_ref[...] = apply(inverse_factor(inner(begin)), begin)
    arrived(1, r2)
    ag[mine] = pk[mine] + jnp.sum(r2[...], axis=0)
    for steps in others:
        send(2, ag.at[mine], ag.at[mine], peer(*steps)[1])
    arrived(2, r2)
    send(3, ag.at[half], ag.at[half], sibling)
    arrived(3, r1)
    for n, out in enumerate((g0, g1, g2, g3)):
        out[...] = ag[32 * n : 32 * n + 32]

    for phase, ref in enumerate((r1, r2, r2, r1)):
        pltpu.make_async_copy(ref, ref, ex_send.at[phase]).wait()

    def sent(j, carry):
        for copy in halo(j):
            copy.wait_send()
        return carry

    lax.fori_loop(0, CHUNKS - 1, sent, 0)
    for j in (CHUNKS - 1, CHUNKS):
        sent(j, 0)
    f_copy.wait()


def iterate_kernel(g0, g1, g2, g3, first_ref, f_hbm, proj_hbm, scores_hbm, gf, gh, gm, gl, tt, fs, sc, pj, f_sem, o_sem, p_sem):
    f_copy = pltpu.make_async_copy(f_hbm, fs, f_sem)
    f_copy.start()

    gf[BP:512, :] = jnp.zeros((512 - BP, 512), F32)
    for t, (rt, ct) in enumerate(LOWER):
        tile = (g0, g1, g2, g3)[t // 32][t % 32]
        if rt == 53 or ct == 3:
            ri, ci = iotas((8, 128))
            tile = jnp.where((ri + 8 * rt < BANDS) & (ci + 128 * ct < BANDS), tile, 0.0)
        gf[8 * rt : 8 * rt + 8, 128 * ct : 128 * ct + 128] = tile
    for i in range(4):
        for j in range(i):
            gf[128 * j : 128 * j + 128, 128 * i : 128 * i + 128] = gf[
                128 * i : 128 * i + 128, 128 * j : 128 * j + 128
            ].T
    for ref, part in zip((gh, gm, gl), split3(gf[...])):
        ref[...] = part

    tt[...] = dot6(first_ref[...], (gh[...], gm[...], gl[...]), NN)

    def step(i, carry):
        t = tt[...]
        s = inner(t)
        z = dot6(t, (gh[...], gm[...], gl[...]), NN)
        tt[...] = apply(inverse_factor(s), z)
        return carry

    lax.fori_loop(1, ITERS, step, 0)
    t = tt[...]
    basis = apply(inverse_factor(inner(t)), t)

    h, m, l = split3(basis)
    lhs = jnp.concatenate([h, h, m, m], axis=0).astype(F32).T.astype(BF16)
    rhs = jnp.concatenate([h, m, h, m], axis=0)
    proj = jnp.dot(lhs, rhs, preferred_element_type=F32)
    pj[...] = proj[0:BANDS, 0:BANDS]
    p_copy = pltpu.make_async_copy(pj, proj_hbm, p_sem)
    p_copy.start()

    f_copy.wait()
    narrow = h[:, 0:BP]

    out = [
        pltpu.make_async_copy(
            sc.at[pl.ds(RANK * ROWS * i, RANK * ROWS)], scores_hbm.at[:, pl.ds(128 * i, 128)], o_sem.at[i]
        )
        for i in range(3)
    ]
    for i in range(3):
        for r in range(ROWS):
            col = r * COLS + 128 * i
            part = jnp.dot(narrow, fs[:, col : col + 128], preferred_element_type=F32)
            sc[pl.ds(RANK * ROWS * i + r, RANK, stride=ROWS), :] = part
        out[i].start()
    for copy in out:
        copy.wait()
    p_copy.wait()


def second(tiles, begin, features):
    vmem = pl.BlockSpec(memory_space=pltpu.VMEM)
    hbm = pl.BlockSpec(memory_space=pltpu.HBM)
    dma = pltpu.SemaphoreType.DMA
    return pl.pallas_call(
        iterate_kernel,
        out_shape=(
            jax.ShapeDtypeStruct((BANDS, BANDS), F32),
            jax.ShapeDtypeStruct((RANK * ROWS, COLS), F32),
        ),
        in_specs=[*[vmem] * 5, hbm],
        out_specs=(hbm, hbm),
        scratch_shapes=[
            pltpu.VMEM((512, 512), F32),
            pltpu.VMEM((512, 512), BF16),
            pltpu.VMEM((512, 512), BF16),
            pltpu.VMEM((512, 512), BF16),
            pltpu.VMEM((RANK, 512), F32),
            pltpu.VMEM((BP, ROWS * COLS), BF16),
            pltpu.VMEM((3 * RANK * ROWS, 128), F32),
            pltpu.VMEM((BANDS, BANDS), F32),
            dma,
            dma((3,)),
            dma,
        ],
        compiler_params=pltpu.CompilerParams(vmem_limit_bytes=54528 * 1024),
    )(*tiles, begin, features)


def first(counts, x, start):
    vmem = pl.BlockSpec(memory_space=pltpu.VMEM)
    hbm = pl.BlockSpec(memory_space=pltpu.HBM)
    dma = pltpu.SemaphoreType.DMA
    return pl.pallas_call(
        features_kernel,
        out_shape=(
            jax.ShapeDtypeStruct((BP, ROWS * COLS), BF16),
            *[jax.ShapeDtypeStruct((32, 8, 128), F32)] * 4,
            jax.ShapeDtypeStruct((RANK, 512), F32),
        ),
        in_specs=[pl.BlockSpec(memory_space=pltpu.SMEM), hbm, hbm],
        out_specs=(hbm, *[vmem] * 5),
        scratch_shapes=[
            pltpu.VMEM((ROWS * (BP + 2), COLS), BF16),
            pltpu.VMEM((HR, COLS), BF16),
            pltpu.VMEM((HR, COLS), BF16),
            pltpu.VMEM((HR, COLS), BF16),
            pltpu.VMEM((HR, COLS), BF16),
            pltpu.VMEM((BP, ROWS * COLS), BF16),
            pltpu.VMEM((192 * CHUNK, COLS), BF16),
            pltpu.VMEM((192 * CHUNK, COLS), BF16),
            pltpu.VMEM((768, 256), BF16),
            pltpu.VMEM((512, 128), BF16),
            pltpu.VMEM((4, BP, COLS), F32),
            pltpu.VMEM((BP, 512), F32),
            pltpu.VMEM((128, 8, 128), F32),
            pltpu.VMEM((64, 8, 128), F32),
            pltpu.VMEM((63, 8, 128), F32),
            pltpu.VMEM((128, 8, 128), F32),
            pltpu.VMEM((RANK, BANDS), F32),
            dma((CHUNKS,)),
            dma,
            dma((CHUNKS + 1,)),
            dma((CHUNKS + 1,)),
            dma((CHUNKS + 1,)),
            dma((CHUNKS + 1,)),
            dma((4,)),
            dma((4,)),
            pltpu.SemaphoreType.REGULAR((2,)),
            dma,
        ],
        compiler_params=pltpu.CompilerParams(
            collective_id=0, has_side_effects=True, vmem_limit_bytes=54528 * 1024
        ),
    )(counts, x, start.T)


def on_device(radiance, counts, start):
    x = radiance.reshape(BANDS * ROWS, COLS)
    features, *tiles, begin = first(counts, x, start)
    projector, scores = second(tiles, begin, features)
    return projector, scores.reshape(1, RANK, ROWS, COLS)


def solution(mesh):
    return jax.shard_map(
        on_device,
        mesh=mesh,
        in_specs=(P("line", None, "track", None), P("line", "track"), P()),
        out_specs=(P(), P("line", None, "track", None)),
        check_vma=False,
    )
```
